256 devices in a mesh: tm: 32 (over x, y, z_hi), space: 8 (over z_lo, core).
Axes of the slice: x: 4, y: 4, z: 8 (z_hi: 2, z_lo: 4; z = z_hi * 4 + z_lo), core: 2. Of those that a mesh axis runs over, the one named last changes fastest.
Arguments:
- coarse_guess: float32 [32, 64, 32, 256], P('tm', 'space'), may hold values from 0 to 2
- initial: float32 [64, 32, 256], P('space'), may hold values from 0 to 2
- kappa: float32 [64, 32, 256], P('space'), may hold values from 0.2 to 2
- source: float32 [64, 32, 256], P('space'), may hold values from -0.5 to 1.5
Outputs:
- fine_states: float32 [128, 64, 32, 256], P('tm', 'space')
- point_change: float32 [32, 64, 32, 256], P('tm', 'space')
The draws below stay inside these ranges and needn't reach their ends.
All inputs are finite; a program needn't handle non-finite values.
Results may differ from the reference program's by a relative error of at most 0.00002.
Values sent between devices are 32-bit elements; how exact they have to be, the bound alone decides.
A program may use at most 64 MiB of HBM per device.

```python
import math
import jax
import jax.numpy as jnp
from jax import lax

NX = 32
NY = 256
STEPS_DEV = 4
SWEEPS = 3
NZ = 64
N_TM = 32


def levels(stream_key, dims, split, smallest, high):
    level, own = 1.0, jax.random.fold_in(stream_key, 6)
    for axis_at, parts in split:
        draws = jnp.exp(jax.random.uniform(jax.random.fold_in(own, axis_at), (parts,), jnp.float32, smallest / len(split), high / len(split)))
        level = level * jnp.repeat(draws, dims[axis_at] // parts).reshape([-1 if axis == axis_at else 1 for axis in range(len(dims))])
    return level


def setup_inputs(seed: int = 0) -> dict:
    streams_of = jax.random.split(jax.random.key(seed), 5)
    return {
        "coarse_guess": jnp.clip(2.0 * jax.random.uniform(streams_of[0], (N_TM, NZ, NX, NY), jnp.float32) ** levels(streams_of[0], (N_TM, NZ, NX, NY), ((0, 32), (1, 8)), -0.2, 0.2), 0.0, 2.0),
        "initial": jnp.clip(2.0 * jax.random.uniform(streams_of[1], (NZ, NX, NY), jnp.float32) ** levels(streams_of[1], (NZ, NX, NY), ((0, 8),), -0.2, 0.2), 0.0, 2.0),
        "kappa": jnp.clip(jnp.exp(math.log(2.0) - 2.3025851 * jax.random.uniform(streams_of[2], (NZ, NX, NY), jnp.float32) ** levels(streams_of[2], (NZ, NX, NY), ((0, 8),), -0.2, 0.2)), 0.2, 2.0),
        "source": jnp.clip(-0.5 + 2.0 * jax.random.uniform(streams_of[3], (NZ, NX, NY), jnp.float32) ** levels(streams_of[3], (NZ, NX, NY), ((0, 8),), -0.2, 0.2), -0.5, 1.5),
    }


step_length = 0.5


def neighbours(field):
    return [field[2:, 1:-1, 1:-1], field[:-2, 1:-1, 1:-1], field[1:-1, 2:, 1:-1],
            field[1:-1, :-2, 1:-1], field[1:-1, 1:-1, 2:], field[1:-1, 1:-1, :-2]]


def jacobi_sweep(state_ext, kappa_ext, right_part, time_step):
    padded_state = jnp.pad(state_ext, ((0, 0), (1, 1), (1, 1)))
    padded_kappa = jnp.pad(kappa_ext, ((0, 0), (1, 1), (1, 1)))
    conduct = padded_kappa * (1.0 + padded_state * padded_state)
    centre = conduct[1:-1, 1:-1, 1:-1]
    weights = jnp.zeros_like(right_part)
    inflow = jnp.zeros_like(right_part)
    for near_k, near_u in zip(neighbours(conduct), neighbours(padded_state)):
        face_value = 0.5 * (centre + near_k)
        weights = weights + face_value
        inflow = inflow + face_value * near_u
    return (right_part + time_step * inflow) / (1.0 + time_step * weights)


def propagate(state_now, kappa, source, time_step):
    right_part = state_now + time_step * source
    kappa_ext = jnp.pad(kappa, ((1, 1), (0, 0), (0, 0)))
    current = state_now
    for repeat in range(SWEEPS):
        current = jacobi_sweep(jnp.pad(current, ((1, 1), (0, 0), (0, 0))), kappa_ext, right_part, time_step)
    return current


def reference(coarse_guess, initial, kappa, source):
    fine_step = step_length
    coarse_step = STEPS_DEV * step_length
    every_slab = jax.vmap(propagate, in_axes=(0, None, None, None))
    prior_state = jnp.concatenate([initial[None], coarse_guess[:-1]], 0)
    relaxed = prior_state
    for repeat in range(STEPS_DEV):
        relaxed = every_slab(relaxed, kappa, source, fine_step)
    fresh_state = jnp.concatenate([initial[None], relaxed[:-1]], 0)
    target = fresh_state
    for repeat in range(STEPS_DEV):
        target = every_slab(target, kappa, source, fine_step)
    coarse_terms = target - every_slab(fresh_state, kappa, source, coarse_step)

    def advance(state_now, term):
        stepped = propagate(state_now, kappa, source, coarse_step) + term
        return stepped, (state_now, stepped)

    finished, (before, own_state) = lax.scan(advance, initial, coarse_terms)
    pieces = []
    current = before
    for repeat in range(STEPS_DEV - 1):
        current = every_slab(current, kappa, source, fine_step)
        pieces.append(current)
    pieces.append(own_state)
    stacked = jnp.stack(pieces, 1)
    return stacked.reshape((STEPS_DEV * N_TM,) + initial.shape), own_state - relaxed
```

```python
import functools

import jax
import jax.numpy as jnp
from jax import lax
from jax.experimental import pallas as pl
from jax.experimental.pallas import tpu as pltpu
from jax.sharding import PartitionSpec as P

MESH = pl.DeviceIdType.MESH
STEPS_DEV = 4
SWEEPS = 3
FINE_STEP = 0.5
COARSE_STEP = STEPS_DEV * FINE_STEP
H = SWEEPS
WINDOW = 6


def kernel(
    n_tm, n_sp, cg, u0, kap, src, fine, pc,
    V, F, KP, HS, T1, T2, K, G, NAT, CT, CTB, REL, OWN,
    cs_sem, cr_sem, hs_sem, hr_sem, fs_sem, fr_sem,
    rel_s, rel_r, bef_s, bef_r, own_s, own_r, ct_s, ct_r, credit,
):
    depth, nx, ny = u0.shape
    xf_n = nx // 8
    half = ny // 2
    top = depth + 2 * H
    t, s = lax.axis_index("tm"), lax.axis_index("space")
    home = n_tm - 1
    is_home = t == home
    has_lo, has_hi = s > 0, s < n_sp - 1
    sides = ((0, has_lo, s - 1), (1, has_hi, s + 1))
    t_next, t_prev = lax.rem(t + 1, n_tm), lax.rem(t + n_tm - 1, n_tm)
    inner = pl.ds(H, depth)

    barrier = pltpu.get_barrier_semaphore()

    def greet(tt, ss):
        pl.semaphore_signal(barrier, inc=1, device_id=(tt, ss), device_id_type=MESH)

    for _, there, ss in sides:
        @pl.when(there)
        def _():
            greet(t, ss)
    greet(t_next, s)
    greet(t_prev, s)

    @pl.when(is_home)
    def _():
        def one(i, c):
            greet(i, s)
            return c
        lax.fori_loop(0, home, one, 0)

    @pl.when(jnp.logical_not(is_home))
    def _():
        greet(home, s)

    row = lax.broadcasted_iota(jnp.int32, (ny, ny), 0)
    col = lax.broadcasted_iota(jnp.int32, (ny, ny), 1)
    want = jnp.where(col < half, 2 * col, 2 * (col - half) + 1)
    split_y = jnp.where(row == want, 1.0, 0.0)
    want_t = jnp.where(row < half, 2 * row, 2 * (row - half) + 1)
    join_y = jnp.where(col == want_t, 1.0, 0.0)

    def permute(rows, matrix):
        return jnp.dot(rows, matrix, precision=lax.Precision.HIGHEST, preferred_element_type=jnp.float32)

    def to_inside(value, put):
        moved = permute(value.reshape(depth * nx, ny), split_y)
        for h in range(2):
            NAT[h] = moved[:, h * half : (h + 1) * half].reshape(depth, nx, half)
        for z in range(depth):
            for xf in range(xf_n):
                for h in range(2):
                    put(z, xf, h, NAT[h, z, pl.ds(xf, 8, stride=xf_n), :])

    def to_outside(get, out):
        for z in range(depth):
            for xf in range(xf_n):
                for h in range(2):
                    NAT[h, z, pl.ds(xf, 8, stride=xf_n), :] = get(z, xf, h)
        rows = jnp.concatenate([NAT[0].reshape(depth * nx, half), NAT[1].reshape(depth * nx, half)], axis=1)
        out[...] = permute(rows, join_y).reshape(depth, nx, ny)

    def lanes(h):
        return slice(h * half, (h + 1) * half)

    def put_start(z, xf, h, x):
        V[0, H + z, xf, :, lanes(h)] = x

    def put_first(z, xf, h, x):
        F[0, H + z, xf, :, lanes(h)] = x

    def put_kap(z, xf, h, x):
        KP[0, H + z, xf, :, lanes(h)] = (0.5 * FINE_STEP) * x

    def put_src(z, xf, h, x):
        HS[0, H + z, xf, :, lanes(h)] = FINE_STEP * x

    to_inside(jnp.where(is_home, u0[...], cg[0]), put_start)
    to_inside(kap[...], put_kap)
    to_inside(src[...], put_src)

    def blank(lo):
        zero = jnp.zeros((H,) + KP.shape[2:], jnp.float32)
        KP[0, pl.ds(lo, H)] = zero
        HS[0, pl.ds(lo, H)] = zero

        def one(i, c):
            V[i, pl.ds(lo, H)] = zero
            return c
        lax.fori_loop(0, V.shape[0], one, 0)

        def two(i, c):
            F[i, pl.ds(lo, H)] = zero
            return c
        lax.fori_loop(0, F.shape[0], two, 0)

    @pl.when(jnp.logical_not(has_lo))
    def _():
        blank(0)

    @pl.when(jnp.logical_not(has_hi))
    def _():
        blank(H + depth)

    greeted = has_lo.astype(jnp.int32) + has_hi.astype(jnp.int32) + 2 + jnp.where(is_home, home, 1)
    pl.semaphore_wait(barrier, greeted)

    def edge(buf, side):
        own = buf.at[pl.ds(H, H)] if side == 0 else buf.at[pl.ds(depth, H)]
        far = buf.at[pl.ds(H + depth, H)] if side == 0 else buf.at[pl.ds(0, H)]
        near = buf.at[pl.ds(0, H)] if side == 0 else buf.at[pl.ds(H + depth, H)]
        return own, far, near

    def halo(buf, send, recv, start):
        for side, there, ss in sides:
            own, far, near = edge(buf, side)

            @pl.when(there)
            def _():
                if start:
                    pltpu.make_async_remote_copy(
                        src_ref=own, dst_ref=far, send_sem=send.at[side], recv_sem=recv.at[1 - side],
                        device_id=(t, ss), device_id_type=MESH).start()
                else:
                    copy = pltpu.make_async_remote_copy(
                        src_ref=own, dst_ref=near, send_sem=send.at[side], recv_sem=recv.at[side],
                        device_id=(t, ss), device_id_type=MESH)
                    copy.wait_send()
                    copy.wait_recv()

    halo(V.at[0], hs_sem.at[0], hr_sem.at[0], True)
    halo(KP.at[0], cs_sem.at[0], cr_sem.at[0], True)
    halo(HS.at[0], cs_sem.at[1], cr_sem.at[1], True)

    lane = lax.broadcasted_iota(jnp.int32, (8, half), 1)
    sub = lax.broadcasted_iota(jnp.int32, (8, half), 0)
    l_first, l_last, s_first, s_last = lane == 0, lane == half - 1, sub == 0, sub == 7
    mask_lo = jnp.where(has_lo, 1.0, 0.0)
    mask_hi = jnp.where(has_hi, 1.0, 0.0)

    def conduct(U, coef, which, z):
        for xf in range(xf_n):
            v, kp = U[z, xf], KP[coef, z, xf]
            k = kp + kp * (v * v)
            K[which, z, xf] = k
            G[which, z, xf] = k * v

    def around(A, z):
        c = [[A[z, xf, :, lanes(h)] for h in range(2)] for xf in range(xf_n)]
        sums = []
        for xf in range(xf_n):
            even, odd = c[xf]
            left = jnp.where(l_first, 0.0, pltpu.roll(odd, 1, 1))
            right = jnp.where(l_last, 0.0, pltpu.roll(even, half - 1, 1))
            along = (left + odd, even + right)
            both = []
            for h in range(2):
                up = c[xf - 1][h] if xf > 0 else jnp.where(s_first, 0.0, pltpu.roll(c[-1][h], 1, 0))
                down = c[xf + 1][h] if xf < xf_n - 1 else jnp.where(s_last, 0.0, pltpu.roll(c[0][h], 7, 0))
                both.append((A[z - 1, xf, :, lanes(h)] + A[z + 1, xf, :, lanes(h)]) + (up + down) + along[h])
            sums.append(both)
        return c, sums

    def relax(U, U0, coef, which, z, out, masked):
        kc, ks = around(K.at[which], z)
        _, vs = around(U, z)
        _, gs = around(G.at[which], z)
        if masked:
            keep = jnp.where(z < H, mask_lo, jnp.where(z >= H + depth, mask_hi, 1.0))
        for xf in range(xf_n):
            for h in range(2):
                k = kc[xf][h]
                right_part = U0[z, xf, :, lanes(h)] + HS[coef, z, xf, :, lanes(h)]
                num = (right_part + gs[xf][h]) + k * vs[xf][h]
                den = (1.0 + ks[xf][h]) + 6.0 * k
                r = pltpu.reciprocal(den, approx=True)
                r = r * (2.0 - den * r)
                value = num * r
                out[z, xf, :, lanes(h)] = value * keep if masked else value

    def span(body, starts, count, unroll):
        def one(i, c):
            for z in starts:
                body(z + i)
            return c
        lax.fori_loop(0, count, one, 0, unroll=unroll)

    last = H + depth

    def early(U, coef, out):
        span(lambda z: conduct(U, coef, 0, z), (H, H + depth // 2), depth // 2, 2)
        span(lambda z: relax(U, U, coef, 0, z, T1, False), (H + 1, H + depth // 2), depth // 2 - 1, 1)
        span(lambda z: conduct(T1, coef, 1, z), (H + 1, H + depth // 2), depth // 2 - 1, 3)
        span(lambda z: relax(T1, U, coef, 1, z, T2, False), (H + 2, H + depth // 2), depth // 2 - 2, 1)
        span(lambda z: conduct(T2, coef, 2, z), (H + 2, H + depth // 2), depth // 2 - 2, 2)
        span(lambda z: relax(T2, U, coef, 2, z, out, False), (H + 3, H + depth // 2), depth // 2 - 3, 1)

    def late(U, coef, out):
        span(lambda z: conduct(U, coef, 0, z), (0, last), H, H)
        span(lambda z: relax(U, U, coef, 0, z, T1, True), (1, last - 1), H, 1)
        span(lambda z: conduct(T1, coef, 1, z), (1, last - 1), H, H)
        span(lambda z: relax(T1, U, coef, 1, z, T2, True), (2, last - 2), H, 1)
        span(lambda z: conduct(T2, coef, 2, z), (2, last - 2), H, H)
        span(lambda z: relax(T2, U, coef, 2, z, out, False), (3, last - 3), H, 1)

    def each(body):
        def one(z, c):
            for xf in range(xf_n):
                body(z, xf)
            return c
        lax.fori_loop(0, depth, one, 0, unroll=2)

    early(V.at[0], 0, V.at[1])
    halo(KP.at[0], cs_sem.at[0], cr_sem.at[0], False)
    halo(HS.at[0], cs_sem.at[1], cr_sem.at[1], False)
    halo(V.at[0], hs_sem.at[0], hr_sem.at[0], False)

    def scale(z, c):
        for xf in range(xf_n):
            KP[1, z, xf] = STEPS_DEV * KP[0, z, xf]
            HS[1, z, xf] = STEPS_DEV * HS[0, z, xf]
        return c
    lax.fori_loop(0, top, scale, 0, unroll=2)
    late(V.at[0], 0, V.at[1])

    def step(n, c):
        par = lax.rem(n, 2)
        halo(V.at[n], hs_sem.at[par], hr_sem.at[par], True)

        @pl.when(n == STEPS_DEV + 1)
        def _():
            U = V.at[STEPS_DEV]
            early(U, 1, F.at[1])
            late(U, 1, F.at[1])

            def keep(z, xf):
                CT[z, xf] = F[1, H + z, xf]
            each(keep)
        early(V.at[n], 0, V.at[n + 1])
        halo(V.at[n], hs_sem.at[par], hr_sem.at[par], False)
        late(V.at[n], 0, V.at[n + 1])
        return c
    lax.fori_loop(1, 2 * STEPS_DEV, step, 0)

    def rel_copy():
        return pltpu.make_async_remote_copy(
            src_ref=V.at[STEPS_DEV, inner], dst_ref=REL, send_sem=rel_s, recv_sem=rel_r,
            device_id=(t_next, s), device_id_type=MESH)

    def ct_copy(i):
        return pltpu.make_async_remote_copy(
            src_ref=CT, dst_ref=CTB.at[i], send_sem=ct_s, recv_sem=ct_r.at[i],
            device_id=(home, s), device_id_type=MESH)

    def bef_copy(n, i):
        return pltpu.make_async_remote_copy(
            src_ref=V.at[n, inner], dst_ref=F.at[0, inner], send_sem=bef_s.at[i], recv_sem=bef_r,
            device_id=(i, s), device_id_type=MESH)

    def own_copy():
        return pltpu.make_async_remote_copy(
            src_ref=F.at[0, inner], dst_ref=OWN, send_sem=own_s, recv_sem=own_r,
            device_id=(t_prev, s), device_id_type=MESH)

    n_terms = n_tm - 2
    first = 2 * STEPS_DEV

    @pl.when(is_home)
    def _():
        rel_copy().start()
        bef_copy(STEPS_DEV, 1).start()

        def advance(i, c):
            n = first + i
            par = lax.rem(n, 2)
            halo(V.at[n], hs_sem.at[par], hr_sem.at[par], True)
            bef_copy(n, i + 2).start()
            early(V.at[n], 1, V.at[n + 1])
            halo(V.at[n], hs_sem.at[par], hr_sem.at[par], False)
            late(V.at[n], 1, V.at[n + 1])
            ct_copy(i).wait_recv()

            def add(z, xf):
                V[n + 1, H + z, xf] = V[n + 1, H + z, xf] + CTB[i, z, xf]
            each(add)

            @pl.when(i + WINDOW < n_terms)
            def _():
                pl.semaphore_signal(credit, inc=1, device_id=(i + WINDOW, s), device_id_type=MESH)
            return c
        lax.fori_loop(0, n_terms - 1, advance, 0)

        def take(z, xf):
            F[0, H + z, xf] = V[first + n_terms - 1, H + z, xf]
        each(take)

    @pl.when(jnp.logical_not(is_home))
    def _():
        @pl.when(t < n_terms)
        def _():
            def term(z, xf):
                CT[z, xf] = V[2 * STEPS_DEV, H + z, xf] - CT[z, xf]
            each(term)

            @pl.when(t >= WINDOW)
            def _():
                pl.semaphore_wait(credit, 1)
            ct_copy(t).start()

        @pl.when(t == n_terms)
        def _():
            rel_copy().start()

        @pl.when(t == 0)
        def _():
            to_inside(u0[...], put_first)

        @pl.when(t > 0)
        def _():
            bef_copy(0, t).wait_recv()

        @pl.when(t != n_terms)
        def _():
            rel_copy().start()

    @pl.when(t > 0)
    def _():
        own_copy().start()

    for i in range(STEPS_DEV - 1):
        par = i % 2
        halo(F.at[i], fs_sem.at[par], fr_sem.at[par], True)
        if i == 1:
            @pl.when(is_home)
            def _():
                early(F.at[0], 1, V.at[0])
                late(F.at[0], 1, V.at[0])
                ct_copy(n_terms - 1).wait_recv()

                def total(z, xf):
                    OWN[z, xf] = V[0, H + z, xf] + CTB[n_terms - 1, z, xf]
                each(total)
        early(F.at[i], 0, F.at[i + 1])
        halo(F.at[i], fs_sem.at[par], fr_sem.at[par], False)
        late(F.at[i], 0, F.at[i + 1])

    for i in range(STEPS_DEV - 1):
        to_outside(lambda z, xf, h: F[i + 1, H + z, xf, :, lanes(h)], fine.at[i])

    @pl.when(jnp.logical_not(is_home))
    def _():
        own_copy().wait_recv()
    rel_copy().wait_recv()
    to_outside(lambda z, xf, h: OWN[z, xf, :, lanes(h)], fine.at[STEPS_DEV - 1])
    to_outside(lambda z, xf, h: OWN[z, xf, :, lanes(h)] - REL[z, xf, :, lanes(h)], pc.at[0])

    rel_copy().wait_send()

    @pl.when(t > 0)
    def _():
        own_copy().wait_send()

    @pl.when(t < n_terms)
    def _():
        ct_copy(t).wait_send()

    @pl.when(is_home)
    def _():
        def one(i, c):
            bef_copy(0, i).wait_send()
            return c
        lax.fori_loop(1, home, one, 0)


def solution(mesh):
    n_tm, n_sp = mesh.shape["tm"], mesh.shape["space"]

    def per_device(coarse_guess, initial, kappa, source):
        depth, nx, ny = initial.shape
        plane = (nx // 8, 8, ny)
        top = depth + 2 * H
        n_terms = n_tm - 2
        dma = pltpu.SemaphoreType.DMA
        whole = pl.BlockSpec(memory_space=pltpu.VMEM)
        f32 = jnp.float32
        return pl.pallas_call(
            functools.partial(kernel, n_tm, n_sp),
            out_shape=(
                jax.ShapeDtypeStruct((STEPS_DEV, depth, nx, ny), f32),
                jax.ShapeDtypeStruct((1, depth, nx, ny), f32),
            ),
            in_specs=[whole] * 4,
            out_specs=(whole, whole),
            scratch_shapes=[
                pltpu.VMEM((2 * STEPS_DEV + n_terms, top) + plane, f32),
                pltpu.VMEM((STEPS_DEV, top) + plane, f32),
                pltpu.VMEM((2, top) + plane, f32),
                pltpu.VMEM((2, top) + plane, f32),
                pltpu.VMEM((top,) + plane, f32),
                pltpu.VMEM((top,) + plane, f32),
                pltpu.VMEM((SWEEPS, top) + plane, f32),
                pltpu.VMEM((SWEEPS, top) + plane, f32),
                pltpu.VMEM((2, depth, nx, ny // 2), f32),
                pltpu.VMEM((depth,) + plane, f32),
                pltpu.VMEM((n_terms, depth) + plane, f32),
                pltpu.VMEM((depth,) + plane, f32),
                pltpu.VMEM((depth,) + plane, f32),
                dma((2, 2)), dma((2, 2)), dma((2, 2)), dma((2, 2)), dma((2, 2)), dma((2, 2)),
                dma, dma, dma((n_tm,)), dma, dma, dma, dma, dma((n_tm,)),
                pltpu.SemaphoreType.REGULAR,
            ],
            compiler_params=pltpu.CompilerParams(
                collective_id=0, has_side_effects=True, vmem_limit_bytes=56 * 1024 * 1024
            ),
        )(coarse_guess, initial, kappa, source)

    return jax.shard_map(
        per_device,
        mesh=mesh,
        in_specs=(
            P("tm", "space", None, None),
            P("space", None, None),
            P("space", None, None),
            P("space", None, None),
        ),
        out_specs=(P("tm", "space", None, None), P("tm", "space", None, None)),
        check_vma=False,
    )
```

```python
import functools

import jax
import jax.numpy as jnp
from jax import lax
from jax.experimental import pallas as pl
from jax.experimental.pallas import tpu as pltpu
from jax.sharding import PartitionSpec as P

MESH = pl.DeviceIdType.MESH
STEPS_DEV = 4
SWEEPS = 3
FINE_STEP = 0.5
COARSE_STEP = STEPS_DEV * FINE_STEP
FAR = 2 * SWEEPS
NEAR = SWEEPS
WINDOW = 8


def kernel(
    n_tm, n_sp, cg, u0, kap, src, fine, pc,
    V, F, KP, HS, T, K, G, NAT, CT, CTB, REL, OWN,
    cf_s, cf_r, vf_s, vf_r, vn_s, vn_r, ff_s, ff_r, fn_s, fn_r,
    rel_s, rel_r, bef_s, bef_r, own_r, ct_s, ct_r, credit,
):
    depth, nx, ny = u0.shape
    xf_n = nx // 8
    half = ny // 2
    top = FAR + depth + NEAR
    t, s = lax.axis_index("tm"), lax.axis_index("space")
    n_slab = n_tm - 2
    zh = lax.rem(t, 2)
    is_home = t >= n_slab
    not_home = t < n_slab
    odd = lax.rem(s, 2)
    near_s = s + 1 - 2 * odd
    far_s = s - 1 + 2 * odd
    has_far = (far_s >= 0) & (far_s < n_sp)
    far_i = has_far.astype(jnp.int32)
    t_next, t_prev = lax.rem(t + 1, n_tm), lax.rem(t + n_tm - 1, n_tm)
    base, sign = odd * (top - 1), 1 - 2 * odd

    def at(p):
        return base + sign * p

    def lowest(p, count):
        return at(p) - odd * (count - 1)

    def layers(p, count):
        return pl.ds(lowest(p, count), count)

    own_lo = lowest(FAR, depth)
    inner = pl.ds(own_lo, depth)

    barrier = pltpu.get_barrier_semaphore()

    def greet(tt, ss):
        pl.semaphore_signal(barrier, inc=1, device_id=(tt, ss), device_id_type=MESH)

    greet(t, near_s)
    greet(t_next, s)
    greet(t_prev, s)

    @pl.when(has_far)
    def _():
        greet(t, far_s)

    @pl.when(is_home)
    def _():
        def one(i, c):
            greet(i, s)

            @pl.when(has_far)
            def _():
                greet(i, far_s)
            return c
        lax.fori_loop(0, n_slab, one, 0)

    @pl.when(not_home)
    def _():
        for h in range(2):
            greet(n_slab + h, s)

            @pl.when(has_far)
            def _():
                greet(n_slab + h, far_s)

    row = lax.broadcasted_iota(jnp.int32, (ny, ny), 0)
    col = lax.broadcasted_iota(jnp.int32, (ny, ny), 1)
    want = jnp.where(col < half, 2 * col, 2 * (col - half) + 1)
    split_y = jnp.where(row == want, 1.0, 0.0)
    want_t = jnp.where(row < half, 2 * row, 2 * (row - half) + 1)
    join_y = jnp.where(col == want_t, 1.0, 0.0)

    def permute(rows, matrix):
        return jnp.dot(rows, matrix, precision=lax.Precision.HIGHEST, preferred_element_type=jnp.float32)

    def lanes(h):
        return slice(h * half, (h + 1) * half)

    def to_inside(value, dst, scale):
        moved = permute(value.reshape(depth * nx, ny), split_y)
        for h in range(2):
            NAT[h] = moved[:, h * half : (h + 1) * half].reshape(depth, nx, half)

        def one(z, c):
            dst[own_lo + z] = jnp.stack([
                jnp.concatenate([scale * NAT[h, z, pl.ds(xf, 8, stride=xf_n), :] for h in range(2)], axis=1)
                for xf in range(xf_n)], axis=0)
            return c
        lax.fori_loop(0, depth, one, 0)

    def to_outside(get, out):
        def one(z, c):
            layer = get(z)
            for xf in range(xf_n):
                for h in range(2):
                    NAT[h, z, pl.ds(xf, 8, stride=xf_n), :] = layer[xf, :, lanes(h)]
            return c
        lax.fori_loop(0, depth, one, 0)
        rows = jnp.concatenate([NAT[0].reshape(depth * nx, half), NAT[1].reshape(depth * nx, half)], axis=1)
        out[...] = permute(rows, join_y).reshape(depth, nx, ny)

    to_inside(jnp.where(is_home, u0[...], cg[0]), V.at[0], 1.0)

    @pl.when(t == n_slab)
    def _():
        to_inside(cg[0], V.at[2 * STEPS_DEV + n_slab + 2], 1.0)
    to_inside(kap[...], KP.at[0], 0.5 * FINE_STEP)
    to_inside(src[...], HS.at[0], FINE_STEP)

    @pl.when(jnp.logical_not(has_far))
    def _():
        zero = jnp.zeros((FAR,) + KP.shape[2:], jnp.float32)
        KP[0, layers(0, FAR)] = zero
        HS[0, layers(0, FAR)] = zero

        def one(i, c):
            V[2 * i, layers(0, FAR)] = zero
            return c
        lax.fori_loop(0, V.shape[0] // 2, one, 0)

        def two(i, c):
            CTB[i, pl.ds(lowest(NEAR, NEAR) - NEAR, NEAR)] = zero[:NEAR]
            return c
        lax.fori_loop(0, n_slab, two, 0)
        for i in (0, 2):
            F[i, layers(0, FAR)] = zero

    greeted = 3 + far_i + jnp.where(is_home, n_slab, 2) * (1 + far_i)
    pl.semaphore_wait(barrier, greeted)

    def remote(src_ref, dst_ref, send, recv, tt, ss):
        return pltpu.make_async_remote_copy(
            src_ref=src_ref, dst_ref=dst_ref, send_sem=send, recv_sem=recv, device_id=(tt, ss), device_id_type=MESH)

    def far_copy(buf, send, recv, j):
        there = (1 - odd) * (top - 1) + (2 * odd - 1) * (FAR - 1 - j)
        return remote(buf.at[at(FAR + j)], buf.at[there], send.at[j], recv.at[j], t, far_s)

    def near_copy(buf, send, recv):
        own = lowest(FAR + depth - NEAR, NEAR)
        there = odd * (top - NEAR)
        return remote(buf.at[pl.ds(own, NEAR)], buf.at[pl.ds(there, NEAR)], send, recv, t, near_s)

    def far_start(buf, send, recv):
        @pl.when(has_far)
        def _():
            for j in range(FAR):
                far_copy(buf, send, recv, j).start()

    def far_wait(buf, send, recv, js):
        @pl.when(has_far)
        def _():
            for j in js:
                copy = far_copy(buf, send, recv, j)
                copy.wait_send()
                copy.wait_recv()

    def near_wait(buf, send, recv):
        copy = near_copy(buf, send, recv)
        copy.wait_send()
        copy.wait_recv()

    near_copy(V.at[0], vn_s.at[0], vn_r.at[0]).start()
    near_copy(KP.at[0], cf_s.at[0, FAR], cf_r.at[0, FAR]).start()
    near_copy(HS.at[0], cf_s.at[1, FAR], cf_r.at[1, FAR]).start()
    far_start(V.at[0], vf_s.at[0], vf_r.at[0])
    far_start(KP.at[0], cf_s.at[0], cf_r.at[0])
    far_start(HS.at[0], cf_s.at[1], cf_r.at[1])

    lane = lax.broadcasted_iota(jnp.int32, (8, half), 1)
    sub = lax.broadcasted_iota(jnp.int32, (8, half), 0)
    l_first, l_last, s_first, s_last = lane == 0, lane == half - 1, sub == 0, sub == 7
    mask_far = jnp.where(has_far, 1.0, 0.0)

    def conduct(U, coef, which, p):
        z = at(p)
        v, kp = U[z], KP[coef, z]
        k = kp + kp * (v * v)
        K[which, z] = k
        G[which, z] = k * v

    def around(A, z):
        here, both_z = A[z], A[z - 1] + A[z + 1]
        c = [[here[xf, :, lanes(h)] for h in range(2)] for xf in range(xf_n)]
        sums = []
        for xf in range(xf_n):
            even_y, odd_y = c[xf]
            left = jnp.where(l_first, 0.0, pltpu.roll(odd_y, 1, 1))
            right = jnp.where(l_last, 0.0, pltpu.roll(even_y, half - 1, 1))
            along = (left + odd_y, even_y + right)
            both = []
            for h in range(2):
                up = c[xf - 1][h] if xf > 0 else jnp.where(s_first, 0.0, pltpu.roll(c[-1][h], 1, 0))
                down = c[xf + 1][h] if xf < xf_n - 1 else jnp.where(s_last, 0.0, pltpu.roll(c[0][h], 7, 0))
                both.append(both_z[xf, :, lanes(h)] + (up + down) + along[h])
            sums.append(both)
        return c, sums

    def relax(U, U0, coef, which, p, out, term, masked):
        z = at(p)
        kc, ks = around(K.at[which], z)
        _, vs = around(U, z)
        _, gs = around(G.at[which], z)
        if masked:
            keep = jnp.where(p < FAR, mask_far, 1.0)
        right_part = U0[z] + HS[coef, z]
        if term is not None:
            extra_term = term[z - NEAR]
        rows = []
        for xf in range(xf_n):
            parts = []
            for h in range(2):
                k = kc[xf][h]
                num = (right_part[xf, :, lanes(h)] + gs[xf][h]) + k * vs[xf][h]
                den = (1.0 + ks[xf][h]) + 6.0 * k
                r = pltpu.reciprocal(den, approx=True)
                r = r * (2.0 - den * r)
                value = num * r
                if masked:
                    value = value * keep
                if term is not None:
                    value = value + extra_term[xf, :, lanes(h)]
                parts.append(value)
            rows.append(jnp.concatenate(parts, axis=1))
        out[z] = jnp.stack(rows, axis=0)

    def span(body, p, count, width):
        turns = count // width
        if turns == 1:
            for k in range(width):
                body(p + k)
        else:
            def one(i, c):
                for k in range(width):
                    body(p + i * width + k)
                return c
            lax.fori_loop(0, turns, one, 0)
        for k in range(turns * width, count):
            body(p + k)

    first, end = FAR, FAR + depth

    def pair(states, n, coefs, terms, waits, far, near):
        U0, U1, U2 = states(n), states(n + 1), states(n + 2)
        far_send, far_recv = far
        near_send, near_recv = near
        c0, c1 = coefs
        term0, term1 = terms
        steps = (
            (U0, c0, (T.at[0], T.at[1], U1), term0),
            (U1, c1, (T.at[2], T.at[3], U2), term1),
        )

        def cond(i, k, p):
            U, c, outs, _ = steps[i]
            conduct(U if k == 0 else outs[k - 1], c, 3 * i + k, p)

        def sweep(i, k, p, masked):
            U, c, outs, term = steps[i]
            relax(U if k == 0 else outs[k - 1], U, c, 3 * i + k, p, outs[k], term if k == 2 else None, masked)

        for i in range(2):
            lo = first + SWEEPS * i
            span(lambda p: cond(i, 0, p), lo, end - lo, 4 if i == 0 else 5)
            span(lambda p: sweep(i, 0, p, False), lo + 1, end - lo - 2, 3)
            near_wait(steps[i][0], near_send.at[i], near_recv.at[i])
            span(lambda p: cond(i, 0, p), end, NEAR, NEAR)
            span(lambda p: sweep(i, 0, p, False), end - 1, NEAR, NEAR)
            span(lambda p: cond(i, 1, p), lo + 1, end + 1 - lo, 3)
            span(lambda p: sweep(i, 1, p, False), lo + 2, end - 1 - lo, 4)
            span(lambda p: cond(i, 2, p), lo + 2, end - 1 - lo, 4)
            waits(i)
            span(lambda p: sweep(i, 2, p, False), lo + 3, end - 3 - lo, 5 if i == 0 else 2)
            if i == 0:
                near_copy(U1, near_send.at[1], near_recv.at[1]).start()

        def wave(j, c):
            @pl.when(has_far)
            def _():
                for k in range(2):
                    copy = far_copy(U0, far_send, far_recv, 2 * j + k)
                    copy.wait_send()
                    copy.wait_recv()
            p = first - 1 - 2 * j
            for i in range(2):
                for k in range(SWEEPS):
                    cond(i, k, p)
                    cond(i, k, p - 1)
                    p = p + 1
                    sweep(i, k, p, True)
                    sweep(i, k, p - 1, True)
            return c
        lax.fori_loop(0, FAR // 2, wave, 0)

    def v_state(n):
        return V.at[n]

    def f_state(n):
        return F.at[n]

    def no_wait(i):
        pass

    def each(body):
        def one(z, c):
            body(z)
            return c
        lax.fori_loop(0, depth, one, 0)

    near_wait(KP.at[0], cf_s.at[0, FAR], cf_r.at[0, FAR])
    near_wait(HS.at[0], cf_s.at[1, FAR], cf_r.at[1, FAR])
    far_wait(KP.at[0], cf_s.at[0], cf_r.at[0], range(FAR))
    far_wait(HS.at[0], cf_s.at[1], cf_r.at[1], range(FAR))

    def scale(z, c):
        KP[1, z] = STEPS_DEV * KP[0, z]
        HS[1, z] = STEPS_DEV * HS[0, z]
        return c
    lax.fori_loop(0, top, scale, 0)

    def v_pair(n, coefs, terms, waits):
        par = lax.rem(lax.div(n, 2), 2)
        pair(v_state, n, coefs, terms, waits, (vf_s.at[par], vf_r.at[par]), (vn_s, vn_r))

    def v_send(n):
        par = lax.rem(lax.div(n, 2), 2)
        near_copy(V.at[n], vn_s.at[0], vn_r.at[0]).start()
        far_start(V.at[n], vf_s.at[par], vf_r.at[par])

    extra = 2 * STEPS_DEV + n_slab + 2

    def fine_pair(m, c):
        n = 2 * m + lax.div(m, STEPS_DEV) * (extra - 2 * STEPS_DEV)

        @pl.when(m > 0)
        def _():
            v_send(n)
        v_pair(n, (0, 0), (None, None), no_wait)

        @pl.when(m == STEPS_DEV // 2)
        def _():
            U = V.at[STEPS_DEV]
            span(lambda p: conduct(U, 1, 0, p), NEAR, top - NEAR, 4)
            span(lambda p: relax(U, U, 1, 0, p, T.at[0], None, True), NEAR + 1, top - NEAR - 2, 4)
            span(lambda p: conduct(T.at[0], 1, 1, p), NEAR + 1, top - NEAR - 2, 4)
            span(lambda p: relax(T.at[0], U, 1, 1, p, T.at[1], None, True), NEAR + 2, top - NEAR - 4, 4)
            span(lambda p: conduct(T.at[1], 1, 2, p), NEAR + 2, top - NEAR - 4, 4)
            span(lambda p: relax(T.at[1], U, 1, 2, p, T.at[2], None, False), first, depth, 4)

            def keep(z):
                CT[z] = T[2, own_lo + z]
            each(keep)
        return c
    lax.fori_loop(0, STEPS_DEV + lax.div(t, n_slab) * (1 - zh) * (STEPS_DEV // 2), fine_pair, 0)

    def rel_copy(n, tt, k):
        return remote(V.at[n, inner], REL, rel_s.at[k], rel_r, tt, s)

    def ct_copy(i, h):
        return remote(CT, CTB.at[i, pl.ds(own_lo - NEAR, depth)], ct_s.at[h, 0], ct_r.at[i, 0], n_slab + h, s)

    def ct_far_copy(i, h):
        mine = odd * (depth - NEAR)
        there = (1 - odd) * depth
        return remote(CT.at[pl.ds(mine, NEAR)], CTB.at[i, pl.ds(there, NEAR)], ct_s.at[h, 1], ct_r.at[i, 1], n_slab + h, far_s)

    def bef_copy(n, i):
        return remote(V.at[n, inner], F.at[0, inner], bef_s.at[i, 0], bef_r, i, s)

    def own_copy(n, i):
        return remote(V.at[n, inner], OWN, bef_s.at[i, 1], own_r, i, s)

    begin = 2 * STEPS_DEV - 1

    def hand_out(d, n):
        to_own = lax.rem(d + zh, 2) == 0

        @pl.when(to_own & (d < n_slab))
        def _():
            own_copy(n, d).start()

        @pl.when(jnp.logical_not(to_own) & (d + 1 < n_slab))
        def _():
            bef_copy(n, d + 1).start()

    def f_pair(n, par):
        near_copy(F.at[n], fn_s.at[0], fn_r.at[0]).start()
        far_start(F.at[n], ff_s.at[par], ff_r.at[par])
        pair(f_state, n, (0, 0), (None, None), no_wait, (ff_s.at[par], ff_r.at[par]), (fn_s, fn_r))

    def f_both(c):
        def one(m, c):
            f_pair(2 * m, m)
            return c
        lax.fori_loop(0, 2, one, 0)

    def take(n):
        def one(z):
            F[0, own_lo + z] = V[n, own_lo + z]
        each(one)

    @pl.when(is_home)
    def _():
        hand_out(0, STEPS_DEV)

        @pl.when(zh == 0)
        def _():
            rel_copy(STEPS_DEV, 0, 0).start()
            rel_copy(extra + STEPS_DEV, t_next, 1).start()

    @pl.when(t == 0)
    def _():
        to_inside(u0[...], F.at[0], 1.0)

    @pl.when(is_home)
    def _():
        def advance(i, c):
            n = 2 * STEPS_DEV + 2 * i
            v_send(n)
            hand_out(2 * i + 1, n)

            def waits(k):
                ct_copy(2 * i + k, 0).wait_recv()
                if k == 0:
                    @pl.when(has_far)
                    def _():
                        ct_far_copy(2 * i, 0).wait_recv()
            v_pair(n, (1, 1), (CTB.at[2 * i], CTB.at[2 * i + 1]), waits)
            hand_out(2 * i + 2, n + 1)
            for k in range(2):
                @pl.when(2 * i + k + WINDOW < n_slab)
                def _():
                    pl.semaphore_signal(
                        credit.at[zh], inc=1, device_id=(2 * i + k + WINDOW, s), device_id_type=MESH)
            return c
        lax.fori_loop(0, n_slab // 2, advance, 0)

        def last(z):
            OWN[z] = V[begin + n_slab + zh, own_lo + z]
        each(last)

    @pl.when(not_home)
    def _():
        def term(z):
            CT[z] = V[2 * STEPS_DEV, own_lo + z] - CT[z]
        each(term)
        for h in range(2):
            @pl.when(t >= WINDOW)
            def _():
                pl.semaphore_wait(credit.at[h], 1)
            ct_copy(t, h).start()

            @pl.when((zh == 0) & has_far)
            def _():
                ct_far_copy(t, h).start()

        @pl.when(t > 0)
        def _():
            bef_copy(0, t).wait_recv()
        rel_copy(STEPS_DEV, t_next, 0).start()

    @pl.when(is_home)
    def _():
        take(begin + n_slab - 1 + zh)
    f_both(0)

    for i in range(STEPS_DEV - 1):
        to_outside(lambda z: F[i + 1, own_lo + z], fine.at[i])

    @pl.when(not_home)
    def _():
        own_copy(0, t).wait_recv()
    rel_copy(STEPS_DEV, t_next, 0).wait_recv()
    to_outside(lambda z: OWN[z], fine.at[STEPS_DEV - 1])
    to_outside(lambda z: OWN[z] - REL[z], pc.at[0])

    @pl.when(not_home)
    def _():
        rel_copy(STEPS_DEV, t_next, 0).wait_send()
        for h in range(2):
            ct_copy(t, h).wait_send()

            @pl.when((zh == 0) & has_far)
            def _():
                ct_far_copy(t, h).wait_send()

    @pl.when(t == n_slab)
    def _():
        for k in range(2):
            rel_copy(STEPS_DEV, 0, k).wait_send()

    @pl.when(is_home)
    def _():
        def one(i, c):
            @pl.when(lax.rem(i + zh, 2) == 0)
            def _():
                own_copy(0, i).wait_send()

                @pl.when(i > 0)
                def _():
                    bef_copy(0, i).wait_send()
            return c
        lax.fori_loop(0, n_slab, one, 0)


def solution(mesh):
    n_tm, n_sp = mesh.shape["tm"], mesh.shape["space"]

    def per_device(coarse_guess, initial, kappa, source):
        depth, nx, ny = initial.shape
        plane = (nx // 8, 8, ny)
        top = FAR + depth + NEAR
        n_terms = n_tm - 2
        dma = pltpu.SemaphoreType.DMA
        whole = pl.BlockSpec(memory_space=pltpu.VMEM)
        f32 = jnp.float32
        return pl.pallas_call(
            functools.partial(kernel, n_tm, n_sp),
            out_shape=(
                jax.ShapeDtypeStruct((STEPS_DEV, depth, nx, ny), f32),
                jax.ShapeDtypeStruct((1, depth, nx, ny), f32),
            ),
            in_specs=[whole] * 4,
            out_specs=(whole, whole),
            scratch_shapes=[
                pltpu.VMEM((3 * STEPS_DEV + 3 + n_terms, top) + plane, f32),
                pltpu.VMEM((STEPS_DEV + 1, top) + plane, f32),
                pltpu.VMEM((2, top) + plane, f32),
                pltpu.VMEM((2, top) + plane, f32),
                pltpu.VMEM((4, top) + plane, f32),
                pltpu.VMEM((2 * SWEEPS, top) + plane, f32),
                pltpu.VMEM((2 * SWEEPS, top) + plane, f32),
                pltpu.VMEM((2, depth, nx, ny // 2), f32),
                pltpu.VMEM((depth,) + plane, f32),
                pltpu.VMEM((n_terms, depth + NEAR) + plane, f32),
                pltpu.VMEM((depth,) + plane, f32),
                pltpu.VMEM((depth,) + plane, f32),
                dma((2, FAR + 1)), dma((2, FAR + 1)),
                dma((2, FAR)), dma((2, FAR)), dma((2,)), dma((2,)),
                dma((2, FAR)), dma((2, FAR)), dma((2,)), dma((2,)),
                dma((2,)), dma, dma((n_tm, 2)), dma, dma, dma((2, 2)), dma((n_tm, 2)),
                pltpu.SemaphoreType.REGULAR((2,)),
            ],
            compiler_params=pltpu.CompilerParams(
                collective_id=0, has_side_effects=True, vmem_limit_bytes=56 * 1024 * 1024
            ),
        )(coarse_guess, initial, kappa, source)

    return jax.shard_map(
        per_device,
        mesh=mesh,
        in_specs=(
            P("tm", "space", None, None),
            P("space", None, None),
            P("space", None, None),
            P("space", None, None),
        ),
        out_specs=(P("tm", "space", None, None), P("tm", "space", None, None)),
        check_vma=False,
    )
```

```python
import functools

import jax
import jax.numpy as jnp
from jax import lax
from jax.experimental import pallas as pl
from jax.experimental.pallas import tpu as pltpu
from jax.sharding import PartitionSpec as P

MESH = pl.DeviceIdType.MESH
STEPS_DEV = 4
SWEEPS = 3
FINE_STEP = 0.5
COARSE_STEP = STEPS_DEV * FINE_STEP
FAR = 2 * SWEEPS
NEAR = SWEEPS
WINDOW = 8


def kernel(
    n_tm, n_sp, cg, u0, kap, src, fine, pc,
    V, F, KP, HS, T, K, G, NAT, CT, CTB, REL, OWN,
    cf_s, cf_r, vf_s, vf_r, vn_s, vn_r, ff_s, ff_r, fn_s, fn_r,
    rel_s, rel_r, bef_s, bef_r, own_r, ct_s, ct_r, th_s, th_r, credit,
):
    depth, nx, ny = u0.shape
    xf_n = nx // 8
    half = ny // 2
    top = FAR + depth + NEAR
    t, s = lax.axis_index("tm"), lax.axis_index("space")
    n_slab = n_tm - 2
    zh = lax.rem(t, 2)
    is_home = t >= n_slab
    not_home = t < n_slab
    odd = lax.rem(s, 2)
    near_s = s + 1 - 2 * odd
    far_s = s - 1 + 2 * odd
    has_far = (far_s >= 0) & (far_s < n_sp)
    far_i = has_far.astype(jnp.int32)
    t_next, t_prev = lax.rem(t + 1, n_tm), lax.rem(t + n_tm - 1, n_tm)
    base, sign = odd * (top - 1), 1 - 2 * odd

    def at(p):
        return base + sign * p

    def lowest(p, count):
        return at(p) - odd * (count - 1)

    def layers(p, count):
        return pl.ds(lowest(p, count), count)

    own_lo = lowest(FAR, depth)
    inner = pl.ds(own_lo, depth)

    barrier = pltpu.get_barrier_semaphore()

    def greet(tt, ss):
        pl.semaphore_signal(barrier, inc=1, device_id=(tt, ss), device_id_type=MESH)

    greet(t, near_s)
    greet(t_next, s)
    greet(t_prev, s)

    @pl.when(has_far)
    def _():
        greet(t, far_s)

    @pl.when(is_home)
    def _():
        def one(i, c):
            greet(i, s)
            return c
        lax.fori_loop(0, n_slab, one, 0)

    @pl.when(not_home)
    def _():
        for h in range(2):
            greet(n_slab + h, s)

    row = lax.broadcasted_iota(jnp.int32, (ny, ny), 0)
    col = lax.broadcasted_iota(jnp.int32, (ny, ny), 1)
    want = jnp.where(col < half, 2 * col, 2 * (col - half) + 1)
    split_y = jnp.where(row == want, 1.0, 0.0)
    want_t = jnp.where(row < half, 2 * row, 2 * (row - half) + 1)
    join_y = jnp.where(col == want_t, 1.0, 0.0)

    def permute(rows, matrix):
        return jnp.dot(rows, matrix, precision=lax.Precision.HIGHEST, preferred_element_type=jnp.float32)

    def lanes(h):
        return slice(h * half, (h + 1) * half)

    def to_inside(value, dst, scale):
        moved = permute(value.reshape(depth * nx, ny), split_y)
        for h in range(2):
            NAT[h] = moved[:, h * half : (h + 1) * half].reshape(depth, nx, half)

        def one(z, c):
            dst[own_lo + z] = jnp.stack([
                jnp.concatenate([scale * NAT[h, z, pl.ds(xf, 8, stride=xf_n), :] for h in range(2)], axis=1)
                for xf in range(xf_n)], axis=0)
            return c
        lax.fori_loop(0, depth, one, 0)

    def to_outside(get, out):
        def one(z, c):
            layer = get(z)
            for xf in range(xf_n):
                for h in range(2):
                    NAT[h, z, pl.ds(xf, 8, stride=xf_n), :] = layer[xf, :, lanes(h)]
            return c
        lax.fori_loop(0, depth, one, 0)
        rows = jnp.concatenate([NAT[0].reshape(depth * nx, half), NAT[1].reshape(depth * nx, half)], axis=1)
        out[...] = permute(rows, join_y).reshape(depth, nx, ny)

    to_inside(jnp.where(is_home, u0[...], cg[0]), V.at[0], 1.0)

    @pl.when(t == n_slab)
    def _():
        to_inside(cg[0], V.at[2 * STEPS_DEV + n_slab + 2], 1.0)
    to_inside(kap[...], KP.at[0], 0.5 * FINE_STEP)
    to_inside(src[...], HS.at[0], FINE_STEP)

    @pl.when(jnp.logical_not(has_far))
    def _():
        zero = jnp.zeros((FAR,) + KP.shape[2:], jnp.float32)
        KP[0, layers(0, FAR)] = zero
        HS[0, layers(0, FAR)] = zero

        def one(i, c):
            V[2 * i, layers(0, FAR)] = zero
            return c
        lax.fori_loop(0, V.shape[0] // 2, one, 0)

        def two(i, c):
            CTB[i, pl.ds(lowest(NEAR, NEAR) - NEAR, NEAR)] = zero[:NEAR]
            return c
        lax.fori_loop(0, n_slab, two, 0)
        for i in (0, 2):
            F[i, layers(0, FAR)] = zero

    greeted = 3 + far_i + jnp.where(is_home, n_slab, 2)
    pl.semaphore_wait(barrier, greeted)

    def remote(src_ref, dst_ref, send, recv, tt, ss):
        return pltpu.make_async_remote_copy(
            src_ref=src_ref, dst_ref=dst_ref, send_sem=send, recv_sem=recv, device_id=(tt, ss), device_id_type=MESH)

    def far_copy(buf, send, recv, j):
        there = (1 - odd) * (top - FAR + 2 * j) + odd * (FAR - 2 - 2 * j)
        return remote(buf.at[layers(FAR + 2 * j, 2)], buf.at[pl.ds(there, 2)], send.at[j], recv.at[j], t, far_s)

    def near_copy(buf, send, recv):
        own = lowest(FAR + depth - NEAR, NEAR)
        there = odd * (top - NEAR)
        return remote(buf.at[pl.ds(own, NEAR)], buf.at[pl.ds(there, NEAR)], send, recv, t, near_s)

    def far_start(buf, send, recv):
        @pl.when(has_far)
        def _():
            for j in range(FAR // 2):
                far_copy(buf, send, recv, j).start()

    def far_wait(buf, send, recv, js):
        @pl.when(has_far)
        def _():
            for j in js:
                copy = far_copy(buf, send, recv, j)
                copy.wait_send()
                copy.wait_recv()

    def near_wait(buf, send, recv):
        copy = near_copy(buf, send, recv)
        copy.wait_send()
        copy.wait_recv()

    near_copy(V.at[0], vn_s.at[0], vn_r.at[0]).start()
    near_copy(KP.at[0], cf_s.at[0, FAR], cf_r.at[0, FAR]).start()
    near_copy(HS.at[0], cf_s.at[1, FAR], cf_r.at[1, FAR]).start()
    far_start(V.at[0], vf_s.at[0], vf_r.at[0])
    far_start(KP.at[0], cf_s.at[0], cf_r.at[0])
    far_start(HS.at[0], cf_s.at[1], cf_r.at[1])

    lane = lax.broadcasted_iota(jnp.int32, (8, half), 1)
    sub = lax.broadcasted_iota(jnp.int32, (8, half), 0)
    l_first, l_last, s_first, s_last = lane == 0, lane == half - 1, sub == 0, sub == 7
    mask_far = jnp.where(has_far, 1.0, 0.0)

    def conduct(U, coef, which, p):
        z = at(p)
        v, kp = U[z], KP[coef, z]
        k = kp + kp * (v * v)
        K[which, z] = k
        G[which, z] = k * v

    def around(A, z):
        here, both_z = A[z], A[z - 1] + A[z + 1]
        c = [[here[xf, :, lanes(h)] for h in range(2)] for xf in range(xf_n)]
        sums = []
        for xf in range(xf_n):
            even_y, odd_y = c[xf]
            left = jnp.where(l_first, 0.0, pltpu.roll(odd_y, 1, 1))
            right = jnp.where(l_last, 0.0, pltpu.roll(even_y, half - 1, 1))
            along = (left + odd_y, even_y + right)
            both = []
            for h in range(2):
                up = c[xf - 1][h] if xf > 0 else jnp.where(s_first, 0.0, pltpu.roll(c[-1][h], 1, 0))
                down = c[xf + 1][h] if xf < xf_n - 1 else jnp.where(s_last, 0.0, pltpu.roll(c[0][h], 7, 0))
                both.append(both_z[xf, :, lanes(h)] + (up + down) + along[h])
            sums.append(both)
        return c, sums

    def relax(U, U0, coef, which, p, out, term, masked):
        z = at(p)
        kc, ks = around(K.at[which], z)
        _, vs = around(U, z)
        _, gs = around(G.at[which], z)
        if masked:
            keep = jnp.where(p < FAR, mask_far, 1.0)
        right_part = U0[z] + HS[coef, z]
        if term is not None:
            extra_term = term[z - NEAR]
        rows = []
        for xf in range(xf_n):
            parts = []
            for h in range(2):
                k = kc[xf][h]
                num = (right_part[xf, :, lanes(h)] + gs[xf][h]) + k * vs[xf][h]
                den = (1.0 + ks[xf][h]) + 6.0 * k
                value = num * pltpu.reciprocal(den, approx=True)
                if masked:
                    value = value * keep
                if term is not None:
                    value = value + extra_term[xf, :, lanes(h)]
                parts.append(value)
            rows.append(jnp.concatenate(parts, axis=1))
        out[z] = jnp.stack(rows, axis=0)

    def span(body, p, count, width):
        turns = count // width
        if turns == 1:
            for k in range(width):
                body(p + k)
        else:
            def one(i, c):
                for k in range(width):
                    body(p + i * width + k)
                return c
            lax.fori_loop(0, turns, one, 0)
        for k in range(turns * width, count):
            body(p + k)

    first, end = FAR, FAR + depth

    def pair(states, n, coefs, terms, waits, far, near, hook, second):
        U0, U1, U2 = states(n), states(n + 1), states(n + 2)
        far_send, far_recv = far
        near_send, near_recv = near
        c0, c1 = coefs
        term0, term1 = terms
        steps = (
            (U0, c0, (T.at[0], T.at[1], U1), term0),
            (U1, c1, (T.at[2], T.at[3], U2), term1),
        )

        def cond(i, k, p):
            U, c, outs, _ = steps[i]
            conduct(U if k == 0 else outs[k - 1], c, 3 * i + k, p)

        def sweep(i, k, p, masked):
            U, c, outs, term = steps[i]
            relax(U if k == 0 else outs[k - 1], U, c, 3 * i + k, p, outs[k], term if k == 2 else None, masked)

        def early(i):
            lo = first + SWEEPS * i
            span(lambda p: cond(i, 0, p), lo, end - lo, 4 if i == 0 else 5)
            span(lambda p: sweep(i, 0, p, False), lo + 1, end - lo - 2, 3)
            near_wait(steps[i][0], near_send.at[i], near_recv.at[i])
            span(lambda p: cond(i, 0, p), end, NEAR, NEAR)
            span(lambda p: sweep(i, 0, p, False), end - 1, NEAR, NEAR)
            span(lambda p: cond(i, 1, p), lo + 1, end + 1 - lo, 3)
            span(lambda p: sweep(i, 1, p, False), lo + 2, end - 1 - lo, 4)
            span(lambda p: cond(i, 2, p), lo + 2, end - 1 - lo, 4)
            waits(i)
            span(lambda p: sweep(i, 2, p, False), lo + 3, end - 3 - lo, 5 if i == 0 else 2)

        early(0)

        def both():
            near_copy(U1, near_send.at[1], near_recv.at[1]).start()
            early(1)
        if second is True:
            both()
        else:
            pl.when(second)(both)
        hook()

        def wave(j, c):
            @pl.when(has_far)
            def _():
                copy = far_copy(U0, far_send, far_recv, j)
                copy.wait_send()
                copy.wait_recv()

            def part(i):
                p = first - 1 - 2 * j + SWEEPS * i
                for k in range(SWEEPS):
                    cond(i, k, p)
                    cond(i, k, p - 1)
                    p = p + 1
                    sweep(i, k, p, True)
                    sweep(i, k, p - 1, True)
            part(0)
            if second is True:
                part(1)
            else:
                pl.when(second)(lambda: part(1))
            return c
        lax.fori_loop(0, FAR // 2, wave, 0)

    def v_state(n):
        return V.at[n]

    def f_state(n):
        return F.at[n]

    def no_wait(i):
        pass

    def each(body):
        def one(z, c):
            body(z)
            return c
        lax.fori_loop(0, depth, one, 0)

    near_wait(KP.at[0], cf_s.at[0, FAR], cf_r.at[0, FAR])
    near_wait(HS.at[0], cf_s.at[1, FAR], cf_r.at[1, FAR])

    def coefficients():
        far_wait(KP.at[0], cf_s.at[0], cf_r.at[0], range(FAR // 2))
        far_wait(HS.at[0], cf_s.at[1], cf_r.at[1], range(FAR // 2))

        def scale(z, c):
            KP[1, z] = STEPS_DEV * KP[0, z]
            HS[1, z] = STEPS_DEV * HS[0, z]
            return c
        lax.fori_loop(0, top, scale, 0)

    def v_pair(n, coefs, terms, waits, hook):
        par = lax.rem(lax.div(n, 2), 2)
        pair(v_state, n, coefs, terms, waits, (vf_s.at[par], vf_r.at[par]), (vn_s, vn_r), hook, True)

    def v_send(n):
        par = lax.rem(lax.div(n, 2), 2)
        near_copy(V.at[n], vn_s.at[0], vn_r.at[0]).start()
        far_start(V.at[n], vf_s.at[par], vf_r.at[par])

    extra = 2 * STEPS_DEV + n_slab + 2

    def fine_pair(m, c):
        n = 2 * m + lax.div(m, STEPS_DEV) * (extra - 2 * STEPS_DEV)

        @pl.when(m > 0)
        def _():
            v_send(n)
        v_pair(n, (0, 0), (None, None), no_wait, lambda: pl.when(m == 0)(coefficients))

        @pl.when(m == STEPS_DEV // 2)
        def _():
            U = V.at[STEPS_DEV]
            span(lambda p: conduct(U, 1, 0, p), NEAR, top - NEAR, 4)
            span(lambda p: relax(U, U, 1, 0, p, T.at[0], None, True), NEAR + 1, top - NEAR - 2, 4)
            span(lambda p: conduct(T.at[0], 1, 1, p), NEAR + 1, top - NEAR - 2, 4)
            span(lambda p: relax(T.at[0], U, 1, 1, p, T.at[1], None, True), NEAR + 2, top - NEAR - 4, 4)
            span(lambda p: conduct(T.at[1], 1, 2, p), NEAR + 2, top - NEAR - 4, 4)
            span(lambda p: relax(T.at[1], U, 1, 2, p, T.at[2], None, False), first, depth, 4)

            def keep(z):
                CT[z] = T[2, own_lo + z]
            each(keep)
        return c
    lax.fori_loop(0, STEPS_DEV + lax.div(t, n_slab) * (1 - zh) * (STEPS_DEV // 2), fine_pair, 0)

    def rel_copy(n, tt, k):
        return remote(V.at[n, inner], REL, rel_s.at[k], rel_r, tt, s)

    def ct_copy(i, h):
        return remote(CT, CTB.at[i, pl.ds(own_lo - NEAR, depth)], ct_s.at[h], ct_r.at[i], n_slab + h, s)

    def halo_copy(i):
        par = lax.rem(i, 2)
        there = (1 - odd) * depth
        return remote(
            CTB.at[2 * i, pl.ds(lowest(FAR, NEAR) - NEAR, NEAR)], CTB.at[2 * i, pl.ds(there, NEAR)],
            th_s.at[par], th_r.at[par], t, far_s)

    def halo_start(i):
        ct_copy(2 * i, 0).wait_recv()

        @pl.when(has_far)
        def _():
            halo_copy(i).start()

    def bef_copy(n, i):
        return remote(V.at[n, inner], F.at[0, inner], bef_s.at[i, 0], bef_r, i, s)

    def own_copy(n, i):
        return remote(V.at[n, inner], OWN, bef_s.at[i, 1], own_r, i, s)

    begin = 2 * STEPS_DEV - 1

    def hand_out(d, n):
        to_own = lax.rem(d + zh, 2) == 0

        @pl.when(to_own & (d < n_slab))
        def _():
            own_copy(n, d).start()

        @pl.when(jnp.logical_not(to_own) & (d + 1 < n_slab))
        def _():
            bef_copy(n, d + 1).start()

    def f_pair(n, par):
        near_copy(F.at[n], fn_s.at[0], fn_r.at[0]).start()
        far_start(F.at[n], ff_s.at[par], ff_r.at[par])
        pair(
            f_state, n, (0, 0), (None, None), no_wait, (ff_s.at[par], ff_r.at[par]), (fn_s, fn_r), lambda: None,
            par == 0)

    def f_both(c):
        def one(m, c):
            f_pair(2 * m, m)
            return c
        lax.fori_loop(0, 2, one, 0)

    def take(n):
        def one(z):
            F[0, own_lo + z] = V[n, own_lo + z]
        each(one)

    @pl.when(is_home)
    def _():
        hand_out(0, STEPS_DEV)

        @pl.when(zh == 0)
        def _():
            rel_copy(STEPS_DEV, 0, 0).start()
            rel_copy(extra + STEPS_DEV, t_next, 1).start()

    @pl.when(t == 0)
    def _():
        to_inside(u0[...], F.at[0], 1.0)

    @pl.when(is_home)
    def _():
        def advance(i, c):
            n = 2 * STEPS_DEV + 2 * i
            v_send(n)
            @pl.when(2 * i + 1 < n_slab - 1)
            def _():
                hand_out(2 * i + 1, n)

            @pl.when(i == 0)
            def _():
                halo_start(i)

            def waits(k):
                if k == 1:
                    ct_copy(2 * i + 1, 0).wait_recv()

            def hook():
                @pl.when(has_far)
                def _():
                    copy = halo_copy(i)
                    copy.wait_send()
                    copy.wait_recv()
            v_pair(n, (1, 1), (CTB.at[2 * i], CTB.at[2 * i + 1]), waits, hook)

            @pl.when(2 * i + 2 < n_slab)
            def _():
                halo_start(i + 1)
            hand_out(2 * i + 2, n + 1)
            for k in range(2):
                @pl.when(2 * i + k + WINDOW < n_slab)
                def _():
                    pl.semaphore_signal(
                        credit.at[zh], inc=1, device_id=(2 * i + k + WINDOW, s), device_id_type=MESH)
            return c
        lax.fori_loop(0, n_slab // 2, advance, 0)
        hand_out(n_slab - 1, begin + n_slab - 1)

        def last(z):
            OWN[z] = V[begin + n_slab + zh, own_lo + z]
        each(last)

    @pl.when(not_home)
    def _():
        def term(z):
            CT[z] = V[2 * STEPS_DEV, own_lo + z] - CT[z]
        each(term)
        for h in range(2):
            @pl.when(t >= WINDOW)
            def _():
                pl.semaphore_wait(credit.at[h], 1)
            ct_copy(t, h).start()

        @pl.when(t >= n_slab - STEPS_DEV)
        def _():
            rel_copy(STEPS_DEV, t_next, 0).start()

        @pl.when(t > 0)
        def _():
            bef_copy(0, t).wait_recv()

        @pl.when(t < n_slab - STEPS_DEV)
        def _():
            rel_copy(STEPS_DEV, t_next, 0).start()

    @pl.when(is_home)
    def _():
        take(begin + n_slab - 1 + zh)
    f_both(0)

    for i in range(STEPS_DEV - 1):
        to_outside(lambda z: F[i + 1, own_lo + z], fine.at[i])

    @pl.when(not_home)
    def _():
        own_copy(0, t).wait_recv()
    rel_copy(STEPS_DEV, t_next, 0).wait_recv()
    to_outside(lambda z: OWN[z], fine.at[STEPS_DEV - 1])
    to_outside(lambda z: OWN[z] - REL[z], pc.at[0])

    @pl.when(not_home)
    def _():
        rel_copy(STEPS_DEV, t_next, 0).wait_send()
        for h in range(2):
            ct_copy(t, h).wait_send()

    @pl.when(t == n_slab)
    def _():
        for k in range(2):
            rel_copy(STEPS_DEV, 0, k).wait_send()

    @pl.when(is_home)
    def _():
        def one(i, c):
            @pl.when(lax.rem(i + zh, 2) == 0)
            def _():
                own_copy(0, i).wait_send()

                @pl.when(i > 0)
                def _():
                    bef_copy(0, i).wait_send()
            return c
        lax.fori_loop(0, n_slab, one, 0)


def solution(mesh):
    n_tm, n_sp = mesh.shape["tm"], mesh.shape["space"]

    def per_device(coarse_guess, initial, kappa, source):
        depth, nx, ny = initial.shape
        plane = (nx // 8, 8, ny)
        top = FAR + depth + NEAR
        n_terms = n_tm - 2
        dma = pltpu.SemaphoreType.DMA
        whole = pl.BlockSpec(memory_space=pltpu.VMEM)
        f32 = jnp.float32
        return pl.pallas_call(
            functools.partial(kernel, n_tm, n_sp),
            out_shape=(
                jax.ShapeDtypeStruct((STEPS_DEV, depth, nx, ny), f32),
                jax.ShapeDtypeStruct((1, depth, nx, ny), f32),
            ),
            in_specs=[whole] * 4,
            out_specs=(whole, whole),
            scratch_shapes=[
                pltpu.VMEM((3 * STEPS_DEV + 3 + n_terms, top) + plane, f32),
                pltpu.VMEM((STEPS_DEV + 1, top) + plane, f32),
                pltpu.VMEM((2, top) + plane, f32),
                pltpu.VMEM((2, top) + plane, f32),
                pltpu.VMEM((4, top) + plane, f32),
                pltpu.VMEM((2 * SWEEPS, top) + plane, f32),
                pltpu.VMEM((2 * SWEEPS, top) + plane, f32),
                pltpu.VMEM((2, depth, nx, ny // 2), f32),
                pltpu.VMEM((depth,) + plane, f32),
                pltpu.VMEM((n_terms, depth + NEAR) + plane, f32),
                pltpu.VMEM((depth,) + plane, f32),
                pltpu.VMEM((depth,) + plane, f32),
                dma((2, FAR + 1)), dma((2, FAR + 1)),
                dma((2, FAR)), dma((2, FAR)), dma((2,)), dma((2,)),
                dma((2, FAR)), dma((2, FAR)), dma((2,)), dma((2,)),
                dma((2,)), dma, dma((n_tm, 2)), dma, dma, dma((2,)), dma((n_tm,)), dma((2,)), dma((2,)),
                pltpu.SemaphoreType.REGULAR((2,)),
            ],
            compiler_params=pltpu.CompilerParams(
                collective_id=0, has_side_effects=True, vmem_limit_bytes=56 * 1024 * 1024
            ),
        )(coarse_guess, initial, kappa, source)

    return jax.shard_map(
        per_device,
        mesh=mesh,
        in_specs=(
            P("tm", "space", None, None),
            P("space", None, None),
            P("space", None, None),
            P("space", None, None),
        ),
        out_specs=(P("tm", "space", None, None), P("tm", "space", None, None)),
        check_vma=False,
    )
```

```python
import functools

import jax
import jax.numpy as jnp
from jax import lax
from jax.experimental import pallas as pl
from jax.experimental.pallas import tpu as pltpu
from jax.sharding import PartitionSpec as P

MESH = pl.DeviceIdType.MESH
STEPS_DEV = 4
SWEEPS = 3
FINE_STEP = 0.5
COARSE_STEP = STEPS_DEV * FINE_STEP
FAR = 2 * SWEEPS
NEAR = SWEEPS
WINDOW = 8


def kernel(
    n_tm, n_sp, cg, u0, kap, src, fine, pc,
    V, F, KP, HS, T, K, G, NAT, CT, CTB, REL, OWN, RB,
    cf_s, cf_r, vf_s, vf_r, vn_s, vn_r, ff_s, ff_r, fn_s, fn_r,
    rel_s, rel_r, bef_s, bef_r, own_r, ct_s, ct_r, th_s, th_r, rb_r, rl_s, credit,
):
    depth, nx, ny = u0.shape
    xf_n = nx // 8
    half = ny // 2
    top = FAR + depth + NEAR
    t, s = lax.axis_index("tm"), lax.axis_index("space")
    n_slab = n_tm - 2
    lane_t = n_tm // 4
    zh = lax.rem(t, 2)
    is_home = t >= n_slab
    not_home = t < n_slab
    odd = lax.rem(s, 2)
    near_s = s + 1 - 2 * odd
    far_s = s - 1 + 2 * odd
    has_far = (far_s >= 0) & (far_s < n_sp)
    far_i = has_far.astype(jnp.int32)
    t_next, t_prev = lax.rem(t + 1, n_tm), lax.rem(t + n_tm - 1, n_tm)
    base, sign = odd * (top - 1), 1 - 2 * odd

    def at(p):
        return base + sign * p

    def lowest(p, count):
        return at(p) - odd * (count - 1)

    def layers(p, count):
        return pl.ds(lowest(p, count), count)

    own_lo = lowest(FAR, depth)
    inner = pl.ds(own_lo, depth)

    barrier = pltpu.get_barrier_semaphore()

    def greet(tt, ss):
        pl.semaphore_signal(barrier, inc=1, device_id=(tt, ss), device_id_type=MESH)

    greet(t, near_s)
    relays, relayed = t < lane_t, (t >= lane_t) & (t < 2 * lane_t)

    @pl.when(relays)
    def _():
        greet(t + lane_t, s)

    @pl.when(relayed)
    def _():
        greet(t - lane_t, s)
    greet(t_next, s)
    greet(t_prev, s)

    @pl.when(has_far)
    def _():
        greet(t, far_s)

    @pl.when(is_home)
    def _():
        def one(i, c):
            greet(i, s)
            return c
        lax.fori_loop(0, n_slab, one, 0)

    @pl.when(not_home)
    def _():
        for h in range(2):
            greet(n_slab + h, s)

    row = lax.broadcasted_iota(jnp.int32, (ny, ny), 0)
    col = lax.broadcasted_iota(jnp.int32, (ny, ny), 1)
    want = jnp.where(col < half, 2 * col, 2 * (col - half) + 1)
    split_y = jnp.where(row == want, 1.0, 0.0)
    want_t = jnp.where(row < half, 2 * row, 2 * (row - half) + 1)
    join_y = jnp.where(col == want_t, 1.0, 0.0)

    def permute(rows, matrix):
        return jnp.dot(rows, matrix, precision=lax.Precision.HIGHEST, preferred_element_type=jnp.float32)

    def lanes(h):
        return slice(h * half, (h + 1) * half)

    def to_inside(value, dst, scale):
        moved = permute(value.reshape(depth * nx, ny), split_y)
        for h in range(2):
            NAT[h] = moved[:, h * half : (h + 1) * half].reshape(depth, nx, half)

        def one(z, c):
            dst[own_lo + z] = jnp.stack([
                jnp.concatenate([scale * NAT[h, z, pl.ds(xf, 8, stride=xf_n), :] for h in range(2)], axis=1)
                for xf in range(xf_n)], axis=0)
            return c
        lax.fori_loop(0, depth, one, 0)

    def to_outside(get, out):
        def one(z, c):
            layer = get(z)
            for xf in range(xf_n):
                for h in range(2):
                    NAT[h, z, pl.ds(xf, 8, stride=xf_n), :] = layer[xf, :, lanes(h)]
            return c
        lax.fori_loop(0, depth, one, 0)
        rows = jnp.concatenate([NAT[0].reshape(depth * nx, half), NAT[1].reshape(depth * nx, half)], axis=1)
        out[...] = permute(rows, join_y).reshape(depth, nx, ny)

    to_inside(jnp.where(is_home, u0[...], cg[0]), V.at[0], 1.0)

    @pl.when(t == n_slab)
    def _():
        to_inside(cg[0], V.at[2 * STEPS_DEV + n_slab + 2], 1.0)
    to_inside(kap[...], KP.at[0], 0.5 * FINE_STEP)
    to_inside(src[...], HS.at[0], FINE_STEP)

    @pl.when(jnp.logical_not(has_far))
    def _():
        zero = jnp.zeros((FAR,) + KP.shape[2:], jnp.float32)
        KP[0, layers(0, FAR)] = zero
        HS[0, layers(0, FAR)] = zero

        def one(i, c):
            V[2 * i, layers(0, FAR)] = zero
            return c
        lax.fori_loop(0, V.shape[0] // 2, one, 0)

        def two(i, c):
            CTB[i, pl.ds(lowest(NEAR, NEAR) - NEAR, NEAR)] = zero[:NEAR]
            return c
        lax.fori_loop(0, n_slab, two, 0)
        for i in (0, 2):
            F[i, layers(0, FAR)] = zero

    greeted = 3 + far_i + jnp.where(is_home, n_slab, 2) + jnp.where(t < 2 * lane_t, 1, 0)
    pl.semaphore_wait(barrier, greeted)

    def remote(src_ref, dst_ref, send, recv, tt, ss):
        return pltpu.make_async_remote_copy(
            src_ref=src_ref, dst_ref=dst_ref, send_sem=send, recv_sem=recv, device_id=(tt, ss), device_id_type=MESH)

    def far_copy(buf, send, recv, j):
        there = (1 - odd) * (top - FAR + 2 * j) + odd * (FAR - 2 - 2 * j)
        return remote(buf.at[layers(FAR + 2 * j, 2)], buf.at[pl.ds(there, 2)], send.at[j], recv.at[j], t, far_s)

    def near_copy(buf, send, recv):
        own = lowest(FAR + depth - NEAR, NEAR)
        there = odd * (top - NEAR)
        return remote(buf.at[pl.ds(own, NEAR)], buf.at[pl.ds(there, NEAR)], send, recv, t, near_s)

    def far_start(buf, send, recv):
        @pl.when(has_far)
        def _():
            for j in range(FAR // 2):
                far_copy(buf, send, recv, j).start()

    def far_wait(buf, send, recv, js):
        @pl.when(has_far)
        def _():
            for j in js:
                copy = far_copy(buf, send, recv, j)
                copy.wait_send()
                copy.wait_recv()

    def near_wait(buf, send, recv):
        copy = near_copy(buf, send, recv)
        copy.wait_send()
        copy.wait_recv()

    near_copy(V.at[0], vn_s.at[0], vn_r.at[0]).start()
    near_copy(KP.at[0], cf_s.at[0, FAR], cf_r.at[0, FAR]).start()
    near_copy(HS.at[0], cf_s.at[1, FAR], cf_r.at[1, FAR]).start()
    far_start(V.at[0], vf_s.at[0], vf_r.at[0])
    far_start(KP.at[0], cf_s.at[0], cf_r.at[0])
    far_start(HS.at[0], cf_s.at[1], cf_r.at[1])

    lane = lax.broadcasted_iota(jnp.int32, (8, half), 1)
    sub = lax.broadcasted_iota(jnp.int32, (8, half), 0)
    l_first, l_last, s_first, s_last = lane == 0, lane == half - 1, sub == 0, sub == 7
    mask_far = jnp.where(has_far, 1.0, 0.0)

    def conduct(U, coef, which, p):
        z = at(p)
        v, kp = U[z], KP[coef, z]
        k = kp + kp * (v * v)
        K[which, z] = k
        G[which, z] = k * v

    def around(A, z):
        here, both_z = A[z], A[z - 1] + A[z + 1]
        c = [[here[xf, :, lanes(h)] for h in range(2)] for xf in range(xf_n)]
        sums = []
        for xf in range(xf_n):
            even_y, odd_y = c[xf]
            left = jnp.where(l_first, 0.0, pltpu.roll(odd_y, 1, 1))
            right = jnp.where(l_last, 0.0, pltpu.roll(even_y, half - 1, 1))
            along = (left + odd_y, even_y + right)
            both = []
            for h in range(2):
                up = c[xf - 1][h] if xf > 0 else jnp.where(s_first, 0.0, pltpu.roll(c[-1][h], 1, 0))
                down = c[xf + 1][h] if xf < xf_n - 1 else jnp.where(s_last, 0.0, pltpu.roll(c[0][h], 7, 0))
                both.append(both_z[xf, :, lanes(h)] + (up + down) + along[h])
            sums.append(both)
        return c, sums

    def relax(U, U0, coef, which, p, out, term, masked):
        z = at(p)
        kc, ks = around(K.at[which], z)
        _, vs = around(U, z)
        _, gs = around(G.at[which], z)
        if masked:
            keep = jnp.where(p < FAR, mask_far, 1.0)
        right_part = U0[z] + HS[coef, z]
        if term is not None:
            extra_term = term[z - NEAR]
        rows = []
        for xf in range(xf_n):
            parts = []
            for h in range(2):
                k = kc[xf][h]
                num = (right_part[xf, :, lanes(h)] + gs[xf][h]) + k * vs[xf][h]
                den = (1.0 + ks[xf][h]) + 6.0 * k
                value = num * pltpu.reciprocal(den, approx=True)
                if masked:
                    value = value * keep
                if term is not None:
                    value = value + extra_term[xf, :, lanes(h)]
                parts.append(value)
            rows.append(jnp.concatenate(parts, axis=1))
        out[z] = jnp.stack(rows, axis=0)

    def span(body, p, count, width):
        turns = count // width
        if turns == 1:
            for k in range(width):
                body(p + k)
        else:
            def one(i, c):
                for k in range(width):
                    body(p + i * width + k)
                return c
            lax.fori_loop(0, turns, one, 0)
        for k in range(turns * width, count):
            body(p + k)

    first, end = FAR, FAR + depth

    def pair(states, n, coefs, terms, waits, far, near, hook, second):
        U0, U1, U2 = states(n), states(n + 1), states(n + 2)
        far_send, far_recv = far
        near_send, near_recv = near
        c0, c1 = coefs
        term0, term1 = terms
        steps = (
            (U0, c0, (T.at[0], T.at[1], U1), term0),
            (U1, c1, (T.at[2], T.at[3], U2), term1),
        )

        def cond(i, k, p):
            U, c, outs, _ = steps[i]
            conduct(U if k == 0 else outs[k - 1], c, 3 * i + k, p)

        def sweep(i, k, p, masked):
            U, c, outs, term = steps[i]
            relax(U if k == 0 else outs[k - 1], U, c, 3 * i + k, p, outs[k], term if k == 2 else None, masked)

        def early(i):
            lo = first + SWEEPS * i
            span(lambda p: cond(i, 0, p), lo, end - lo, 4 if i == 0 else 5)
            span(lambda p: sweep(i, 0, p, False), lo + 1, end - lo - 2, 3)
            near_wait(steps[i][0], near_send.at[i], near_recv.at[i])
            span(lambda p: cond(i, 0, p), end, NEAR, NEAR)
            span(lambda p: sweep(i, 0, p, False), end - 1, NEAR, NEAR)
            span(lambda p: cond(i, 1, p), lo + 1, end + 1 - lo, 3)
            span(lambda p: sweep(i, 1, p, False), lo + 2, end - 1 - lo, 4)
            span(lambda p: cond(i, 2, p), lo + 2, end - 1 - lo, 4)
            waits(i)
            span(lambda p: sweep(i, 2, p, False), lo + 3, end - 3 - lo, 5 if i == 0 else 2)

        early(0)

        def both():
            near_copy(U1, near_send.at[1], near_recv.at[1]).start()
            early(1)
        if second is True:
            both()
        else:
            pl.when(second)(both)
        hook()

        def wave(j, c):
            @pl.when(has_far)
            def _():
                copy = far_copy(U0, far_send, far_recv, j)
                copy.wait_send()
                copy.wait_recv()

            def part(i):
                p = first - 1 - 2 * j + SWEEPS * i
                for k in range(SWEEPS):
                    cond(i, k, p)
                    cond(i, k, p - 1)
                    p = p + 1
                    sweep(i, k, p, True)
                    sweep(i, k, p - 1, True)
            part(0)
            if second is True:
                part(1)
            else:
                pl.when(second)(lambda: part(1))
            return c
        lax.fori_loop(0, FAR // 2, wave, 0)

    def v_state(n):
        return V.at[n]

    def f_state(n):
        return F.at[n]

    def no_wait(i):
        pass

    def each(body):
        def one(z, c):
            body(z)
            return c
        lax.fori_loop(0, depth, one, 0)

    near_wait(KP.at[0], cf_s.at[0, FAR], cf_r.at[0, FAR])
    near_wait(HS.at[0], cf_s.at[1, FAR], cf_r.at[1, FAR])

    def coefficients():
        far_wait(KP.at[0], cf_s.at[0], cf_r.at[0], range(FAR // 2))
        far_wait(HS.at[0], cf_s.at[1], cf_r.at[1], range(FAR // 2))

        def scale(z, c):
            KP[1, z] = STEPS_DEV * KP[0, z]
            HS[1, z] = STEPS_DEV * HS[0, z]
            return c
        lax.fori_loop(0, top, scale, 0)

    def v_pair(n, coefs, terms, waits, hook):
        par = lax.rem(lax.div(n, 2), 2)
        pair(v_state, n, coefs, terms, waits, (vf_s.at[par], vf_r.at[par]), (vn_s, vn_r), hook, True)

    def v_send(n):
        par = lax.rem(lax.div(n, 2), 2)
        near_copy(V.at[n], vn_s.at[0], vn_r.at[0]).start()
        far_start(V.at[n], vf_s.at[par], vf_r.at[par])

    extra = 2 * STEPS_DEV + n_slab + 2

    def fine_pair(m, c):
        n = 2 * m + lax.div(m, STEPS_DEV) * (extra - 2 * STEPS_DEV)

        @pl.when(m > 0)
        def _():
            v_send(n)
        v_pair(n, (0, 0), (None, None), no_wait, lambda: pl.when(m == 0)(coefficients))

        @pl.when(m == STEPS_DEV // 2)
        def _():
            U = V.at[STEPS_DEV]
            span(lambda p: conduct(U, 1, 0, p), NEAR, top - NEAR, 4)
            span(lambda p: relax(U, U, 1, 0, p, T.at[0], None, True), NEAR + 1, top - NEAR - 2, 4)
            span(lambda p: conduct(T.at[0], 1, 1, p), NEAR + 1, top - NEAR - 2, 4)
            span(lambda p: relax(T.at[0], U, 1, 1, p, T.at[1], None, True), NEAR + 2, top - NEAR - 4, 4)
            span(lambda p: conduct(T.at[1], 1, 2, p), NEAR + 2, top - NEAR - 4, 4)
            span(lambda p: relax(T.at[1], U, 1, 2, p, T.at[2], None, False), first, depth, 4)

            def keep(z):
                CT[z] = T[2, own_lo + z]
            each(keep)
        return c
    lax.fori_loop(0, STEPS_DEV + lax.div(t, n_slab) * (1 - zh) * (STEPS_DEV // 2), fine_pair, 0)

    def rel_copy(n, tt, k):
        return remote(V.at[n, inner], REL, rel_s.at[k], rel_r, tt, s)

    def ct_copy(i, h):
        return remote(CT, CTB.at[i, pl.ds(own_lo - NEAR, depth)], ct_s.at[h], ct_r.at[i], n_slab + h, s)

    def halo_copy(i):
        par = lax.rem(i, 2)
        there = (1 - odd) * depth
        return remote(
            CTB.at[2 * i, pl.ds(lowest(FAR, NEAR) - NEAR, NEAR)], CTB.at[2 * i, pl.ds(there, NEAR)],
            th_s.at[par], th_r.at[par], t, far_s)

    def halo_start(i):
        ct_copy(2 * i, 0).wait_recv()

        @pl.when(has_far)
        def _():
            halo_copy(i).start()

    def bef_copy(n, i):
        return remote(V.at[n, inner], F.at[0, inner], bef_s.at[i, 0], bef_r, i, s)

    def own_copy(n, i):
        return remote(V.at[n, inner], OWN, bef_s.at[i, 1], own_r, i, s)

    begin = 2 * STEPS_DEV - 1

    def relay_in(n, i, k):
        return remote(V.at[n, inner], RB.at[k], bef_s.at[i, k], rb_r.at[k], i - lane_t, s)

    def relay_out(k):
        dst, recv = ((F.at[0, inner], bef_r), (OWN, own_r))[k]
        return remote(RB.at[k], dst, rl_s.at[k], recv, t + lane_t, s)

    def hand_out(d, n):
        d = jnp.asarray(d, jnp.int32)
        to_own = lax.rem(d + zh, 2) == 0
        for k, e, wanted in ((0, d + 1, jnp.logical_not(to_own)), (1, d, to_own)):
            wanted = wanted & (e < n_slab)
            by_relay = (e >= lane_t) & (e < 2 * lane_t)

            @pl.when(wanted & by_relay)
            def _():
                relay_in(n, e, k).start()

            @pl.when(wanted & jnp.logical_not(by_relay))
            def _():
                (bef_copy, own_copy)[k](n, e).start()

    def f_pair(n, par):
        near_copy(F.at[n], fn_s.at[0], fn_r.at[0]).start()
        far_start(F.at[n], ff_s.at[par], ff_r.at[par])
        pair(
            f_state, n, (0, 0), (None, None), no_wait, (ff_s.at[par], ff_r.at[par]), (fn_s, fn_r), lambda: None,
            par == 0)

    def f_both(c):
        def one(m, c):
            f_pair(2 * m, m)
            return c
        lax.fori_loop(0, 2, one, 0)

    def take(n):
        def one(z):
            F[0, own_lo + z] = V[n, own_lo + z]
        each(one)

    @pl.when(is_home)
    def _():
        hand_out(0, STEPS_DEV)

        @pl.when(zh == 0)
        def _():
            rel_copy(STEPS_DEV, 0, 0).start()
            rel_copy(extra + STEPS_DEV, t_next, 1).start()

    @pl.when(t == 0)
    def _():
        to_inside(u0[...], F.at[0], 1.0)

    @pl.when(is_home)
    def _():
        def advance(i, c):
            n = 2 * STEPS_DEV + 2 * i
            v_send(n)
            @pl.when(2 * i + 1 < n_slab - 1)
            def _():
                hand_out(2 * i + 1, n)

            @pl.when(i == 0)
            def _():
                halo_start(i)

            def release():
                for k in range(2):
                    @pl.when(2 * i + k + WINDOW < n_slab)
                    def _():
                        pl.semaphore_signal(
                            credit.at[zh], inc=1, device_id=(2 * i + k + WINDOW, s), device_id_type=MESH)

            def waits(k):
                if k == 1:
                    ct_copy(2 * i + 1, 0).wait_recv()
                    release()

            def hook():
                @pl.when(has_far)
                def _():
                    copy = halo_copy(i)
                    copy.wait_send()
                    copy.wait_recv()
            v_pair(n, (1, 1), (CTB.at[2 * i], CTB.at[2 * i + 1]), waits, hook)

            @pl.when(2 * i + 2 < n_slab)
            def _():
                halo_start(i + 1)
            hand_out(2 * i + 2, n + 1)
            return c
        lax.fori_loop(0, n_slab // 2, advance, 0)
        hand_out(n_slab - 1, begin + n_slab - 1)

        def last(z):
            OWN[z] = V[begin + n_slab + zh, own_lo + z]
        each(last)

    @pl.when(not_home)
    def _():
        def term(z):
            CT[z] = V[2 * STEPS_DEV, own_lo + z] - CT[z]
        each(term)
        for h in range(2):
            @pl.when(t >= WINDOW)
            def _():
                pl.semaphore_wait(credit.at[h], 1)
            ct_copy(t, h).start()

        @pl.when(t >= n_slab - STEPS_DEV)
        def _():
            rel_copy(STEPS_DEV, t_next, 0).start()

        @pl.when(t > 0)
        def _():
            bef_copy(0, t).wait_recv()

        @pl.when(t < n_slab - STEPS_DEV)
        def _():
            rel_copy(STEPS_DEV, t_next, 0).start()

    @pl.when(is_home)
    def _():
        take(begin + n_slab - 1 + zh)
    f_both(0)

    for i in range(STEPS_DEV - 1):
        to_outside(lambda z: F[i + 1, own_lo + z], fine.at[i])

    @pl.when(not_home)
    def _():
        own_copy(0, t).wait_recv()
    rel_copy(STEPS_DEV, t_next, 0).wait_recv()
    to_outside(lambda z: OWN[z], fine.at[STEPS_DEV - 1])
    to_outside(lambda z: OWN[z] - REL[z], pc.at[0])

    @pl.when(relays)
    def _():
        for k in range(2):
            relay_in(0, t + lane_t, k).wait_recv()
            relay_out(k).start()
        for k in range(2):
            relay_out(k).wait_send()

    @pl.when(not_home)
    def _():
        rel_copy(STEPS_DEV, t_next, 0).wait_send()
        for h in range(2):
            ct_copy(t, h).wait_send()

    @pl.when(t == n_slab)
    def _():
        for k in range(2):
            rel_copy(STEPS_DEV, 0, k).wait_send()

    @pl.when(is_home)
    def _():
        def one(i, c):
            @pl.when(lax.rem(i + zh, 2) == 0)
            def _():
                own_copy(0, i).wait_send()

                @pl.when(i > 0)
                def _():
                    bef_copy(0, i).wait_send()
            return c
        lax.fori_loop(0, n_slab, one, 0)


def solution(mesh):
    n_tm, n_sp = mesh.shape["tm"], mesh.shape["space"]

    def per_device(coarse_guess, initial, kappa, source):
        depth, nx, ny = initial.shape
        plane = (nx // 8, 8, ny)
        top = FAR + depth + NEAR
        n_terms = n_tm - 2
        dma = pltpu.SemaphoreType.DMA
        whole = pl.BlockSpec(memory_space=pltpu.VMEM)
        f32 = jnp.float32
        return pl.pallas_call(
            functools.partial(kernel, n_tm, n_sp),
            out_shape=(
                jax.ShapeDtypeStruct((STEPS_DEV, depth, nx, ny), f32),
                jax.ShapeDtypeStruct((1, depth, nx, ny), f32),
            ),
            in_specs=[whole] * 4,
            out_specs=(whole, whole),
            scratch_shapes=[
                pltpu.VMEM((3 * STEPS_DEV + 3 + n_terms, top) + plane, f32),
                pltpu.VMEM((STEPS_DEV + 1, top) + plane, f32),
                pltpu.VMEM((2, top) + plane, f32),
                pltpu.VMEM((2, top) + plane, f32),
                pltpu.VMEM((4, top) + plane, f32),
                pltpu.VMEM((2 * SWEEPS, top) + plane, f32),
                pltpu.VMEM((2 * SWEEPS, top) + plane, f32),
                pltpu.VMEM((2, depth, nx, ny // 2), f32),
                pltpu.VMEM((depth,) + plane, f32),
                pltpu.VMEM((n_terms, depth + NEAR) + plane, f32),
                pltpu.VMEM((depth,) + plane, f32),
                pltpu.VMEM((depth,) + plane, f32),
                pltpu.VMEM((2, depth) + plane, f32),
                dma((2, FAR + 1)), dma((2, FAR + 1)),
                dma((2, FAR)), dma((2, FAR)), dma((2,)), dma((2,)),
                dma((2, FAR)), dma((2, FAR)), dma((2,)), dma((2,)),
                dma((2,)), dma, dma((n_tm, 2)), dma, dma, dma((2,)), dma((n_tm,)), dma((2,)), dma((2,)), dma((2,)), dma((2,)),
                pltpu.SemaphoreType.REGULAR((2,)),
            ],
            compiler_params=pltpu.CompilerParams(
                collective_id=0, has_side_effects=True, vmem_limit_bytes=56 * 1024 * 1024
            ),
        )(coarse_guess, initial, kappa, source)

    return jax.shard_map(
        per_device,
        mesh=mesh,
        in_specs=(
            P("tm", "space", None, None),
            P("space", None, None),
            P("space", None, None),
            P("space", None, None),
        ),
        out_specs=(P("tm", "space", None, None), P("tm", "space", None, None)),
        check_vma=False,
    )
```

```python
import functools

import jax
import jax.numpy as jnp
from jax import lax
from jax.experimental import pallas as pl
from jax.experimental.pallas import tpu as pltpu
from jax.sharding import PartitionSpec as P

MESH = pl.DeviceIdType.MESH
STEPS_DEV = 4
SWEEPS = 3
FINE_STEP = 0.5
COARSE_STEP = STEPS_DEV * FINE_STEP
FAR = 2 * SWEEPS
NEAR = SWEEPS
WINDOW = 8


def kernel(
    n_tm, n_sp, cg, u0, kap, src, fine, pc,
    V, F, KP, HS, T, K, G, NAT, CT, CTB, REL, OWN, RB,
    cf_s, cf_r, vf_s, vf_r, vn_s, vn_r, ff_s, ff_r, fn_s, fn_r,
    rel_s, rel_r, bef_s, bef_r, own_r, ct_s, ct_r, th_s, th_r, rb_r, rl_s, credit,
):
    depth, nx, ny = u0.shape
    xf_n = nx // 8
    half = ny // 2
    top = FAR + depth + NEAR
    t, s = lax.axis_index("tm"), lax.axis_index("space")
    n_slab = n_tm - 2
    lane_t = n_tm // 4
    zh = lax.rem(t, 2)
    is_home = t >= n_slab
    not_home = t < n_slab
    odd = lax.rem(s, 2)
    near_s = s + 1 - 2 * odd
    far_s = s - 1 + 2 * odd
    has_far = (far_s >= 0) & (far_s < n_sp)
    far_i = has_far.astype(jnp.int32)
    t_next, t_prev = lax.rem(t + 1, n_tm), lax.rem(t + n_tm - 1, n_tm)
    base, sign = odd * (top - 1), 1 - 2 * odd

    def at(p):
        return base + sign * p

    def lowest(p, count):
        return at(p) - odd * (count - 1)

    def layers(p, count):
        return pl.ds(lowest(p, count), count)

    own_lo = lowest(FAR, depth)
    inner = pl.ds(own_lo, depth)

    barrier = pltpu.get_barrier_semaphore()

    def greet(tt, ss):
        pl.semaphore_signal(barrier, inc=1, device_id=(tt, ss), device_id_type=MESH)

    greet(t, near_s)
    relays, relayed = t < lane_t, (t >= lane_t) & (t < 2 * lane_t)

    @pl.when(relays)
    def _():
        greet(t + lane_t, s)

    @pl.when(relayed)
    def _():
        greet(t - lane_t, s)
    greet(t_next, s)
    greet(t_prev, s)

    @pl.when(has_far)
    def _():
        greet(t, far_s)

    @pl.when(is_home)
    def _():
        def one(i, c):
            greet(i, s)
            return c
        lax.fori_loop(0, n_slab, one, 0)

    @pl.when(not_home)
    def _():
        for h in range(2):
            greet(n_slab + h, s)

    row = lax.broadcasted_iota(jnp.int32, (ny, ny), 0)
    col = lax.broadcasted_iota(jnp.int32, (ny, ny), 1)
    want = jnp.where(col < half, 2 * col, 2 * (col - half) + 1)
    split_y = jnp.where(row == want, 1.0, 0.0)
    want_t = jnp.where(row < half, 2 * row, 2 * (row - half) + 1)
    join_y = jnp.where(col == want_t, 1.0, 0.0)

    def permute(rows, matrix):
        return jnp.dot(rows, matrix, precision=lax.Precision.HIGHEST, preferred_element_type=jnp.float32)

    def lanes(h):
        return slice(h * half, (h + 1) * half)

    def to_inside(value, dst, scale):
        moved = permute(value.reshape(depth * nx, ny), split_y)
        for h in range(2):
            NAT[h] = moved[:, h * half : (h + 1) * half].reshape(depth, nx, half)

        def one(z, c):
            dst[own_lo + z] = jnp.stack([
                jnp.concatenate([scale * NAT[h, z, pl.ds(xf, 8, stride=xf_n), :] for h in range(2)], axis=1)
                for xf in range(xf_n)], axis=0)
            return c
        lax.fori_loop(0, depth, one, 0)

    def to_outside(get, out):
        def one(z, c):
            layer = get(z)
            for xf in range(xf_n):
                for h in range(2):
                    NAT[h, z, pl.ds(xf, 8, stride=xf_n), :] = layer[xf, :, lanes(h)]
            return c
        lax.fori_loop(0, depth, one, 0)
        rows = jnp.concatenate([NAT[0].reshape(depth * nx, half), NAT[1].reshape(depth * nx, half)], axis=1)
        out[...] = permute(rows, join_y).reshape(depth, nx, ny)

    to_inside(jnp.where(is_home, u0[...], cg[0]), V.at[0], 1.0)

    @pl.when(t == n_slab)
    def _():
        to_inside(cg[0], V.at[2 * STEPS_DEV + n_slab + 2], 1.0)
    to_inside(kap[...], KP.at[0], 0.5 * FINE_STEP)
    to_inside(src[...], HS.at[0], FINE_STEP)

    @pl.when(jnp.logical_not(has_far))
    def _():
        zero = jnp.zeros((FAR,) + KP.shape[2:], jnp.float32)
        KP[0, layers(0, FAR)] = zero
        HS[0, layers(0, FAR)] = zero

        def one(i, c):
            V[2 * i, layers(0, FAR)] = zero
            return c
        lax.fori_loop(0, V.shape[0] // 2, one, 0)

        def two(i, c):
            CTB[i, pl.ds(lowest(NEAR, NEAR) - NEAR, NEAR)] = zero[:NEAR]
            return c
        lax.fori_loop(0, n_slab, two, 0)
        for i in (0, 2):
            F[i, layers(0, FAR)] = zero

    greeted = 3 + far_i + jnp.where(is_home, n_slab, 2) + jnp.where(t < 2 * lane_t, 1, 0)
    pl.semaphore_wait(barrier, greeted)

    def remote(src_ref, dst_ref, send, recv, tt, ss):
        return pltpu.make_async_remote_copy(
            src_ref=src_ref, dst_ref=dst_ref, send_sem=send, recv_sem=recv, device_id=(tt, ss), device_id_type=MESH)

    def far_copy(buf, send, recv, j):
        there = (1 - odd) * (top - FAR + 2 * j) + odd * (FAR - 2 - 2 * j)
        return remote(buf.at[layers(FAR + 2 * j, 2)], buf.at[pl.ds(there, 2)], send.at[j], recv.at[j], t, far_s)

    def near_copy(buf, send, recv):
        own = lowest(FAR + depth - NEAR, NEAR)
        there = odd * (top - NEAR)
        return remote(buf.at[pl.ds(own, NEAR)], buf.at[pl.ds(there, NEAR)], send, recv, t, near_s)

    def far_start(buf, send, recv):
        @pl.when(has_far)
        def _():
            for j in range(FAR // 2):
                far_copy(buf, send, recv, j).start()

    def far_wait(buf, send, recv, js):
        @pl.when(has_far)
        def _():
            for j in js:
                copy = far_copy(buf, send, recv, j)
                copy.wait_send()
                copy.wait_recv()

    def near_wait(buf, send, recv):
        copy = near_copy(buf, send, recv)
        copy.wait_send()
        copy.wait_recv()

    near_copy(V.at[0], vn_s.at[0], vn_r.at[0]).start()
    near_copy(KP.at[0], cf_s.at[0, FAR], cf_r.at[0, FAR]).start()
    near_copy(HS.at[0], cf_s.at[1, FAR], cf_r.at[1, FAR]).start()
    far_start(V.at[0], vf_s.at[0], vf_r.at[0])
    far_start(KP.at[0], cf_s.at[0], cf_r.at[0])
    far_start(HS.at[0], cf_s.at[1], cf_r.at[1])

    lane = lax.broadcasted_iota(jnp.int32, (8, half), 1)
    sub = lax.broadcasted_iota(jnp.int32, (8, half), 0)
    l_first, l_last, s_first, s_last = lane == 0, lane == half - 1, sub == 0, sub == 7
    mask_far = jnp.where(has_far, 1.0, 0.0)

    def conduct(U, coef, which, p):
        z = at(p)
        v, kp = U[z], KP[coef, z]
        k = kp + kp * (v * v)
        K[which, z] = k
        G[which, z] = k * v

    def around(A, z):
        here, both_z = A[z], A[z - 1] + A[z + 1]
        c = [[here[xf, :, lanes(h)] for h in range(2)] for xf in range(xf_n)]
        sums = []
        for xf in range(xf_n):
            even_y, odd_y = c[xf]
            left = jnp.where(l_first, 0.0, pltpu.roll(odd_y, 1, 1))
            right = jnp.where(l_last, 0.0, pltpu.roll(even_y, half - 1, 1))
            along = (left + odd_y, even_y + right)
            both = []
            for h in range(2):
                up = c[xf - 1][h] if xf > 0 else jnp.where(s_first, 0.0, pltpu.roll(c[-1][h], 1, 0))
                down = c[xf + 1][h] if xf < xf_n - 1 else jnp.where(s_last, 0.0, pltpu.roll(c[0][h], 7, 0))
                both.append(both_z[xf, :, lanes(h)] + (up + down) + along[h])
            sums.append(both)
        return c, sums

    def relax(U, U0, coef, which, p, out, term, masked):
        z = at(p)
        kc, ks = around(K.at[which], z)
        _, vs = around(U, z)
        _, gs = around(G.at[which], z)
        if masked:
            keep = jnp.where(p < FAR, mask_far, 1.0)
        right_part = U0[z] + HS[coef, z]
        if term is not None:
            extra_term = term[z - NEAR]
        rows = []
        for xf in range(xf_n):
            parts = []
            for h in range(2):
                k = kc[xf][h]
                num = (right_part[xf, :, lanes(h)] + gs[xf][h]) + k * vs[xf][h]
                den = (1.0 + ks[xf][h]) + 6.0 * k
                value = num * pltpu.reciprocal(den, approx=True)
                if masked:
                    value = value * keep
                if term is not None:
                    value = value + extra_term[xf, :, lanes(h)]
                parts.append(value)
            rows.append(jnp.concatenate(parts, axis=1))
        out[z] = jnp.stack(rows, axis=0)

    def span(body, p, count, width):
        turns = count // width
        if turns == 1:
            for k in range(width):
                body(p + k)
        else:
            def one(i, c):
                for k in range(width):
                    body(p + i * width + k)
                return c
            lax.fori_loop(0, turns, one, 0)
        for k in range(turns * width, count):
            body(p + k)

    first, end = FAR, FAR + depth

    def pair(states, n, coefs, terms, waits, far, near, hook, second):
        U0, U1, U2 = states(n), states(n + 1), states(n + 2)
        far_send, far_recv = far
        near_send, near_recv = near
        c0, c1 = coefs
        term0, term1 = terms
        steps = (
            (U0, c0, (T.at[0], T.at[1], U1), term0),
            (U1, c1, (T.at[2], T.at[3], U2), term1),
        )

        def cond(i, k, p):
            U, c, outs, _ = steps[i]
            conduct(U if k == 0 else outs[k - 1], c, 3 * i + k, p)

        def sweep(i, k, p, masked):
            U, c, outs, term = steps[i]
            relax(U if k == 0 else outs[k - 1], U, c, 3 * i + k, p, outs[k], term if k == 2 else None, masked)

        def early(i):
            lo = first + SWEEPS * i
            span(lambda p: cond(i, 0, p), lo, end - lo, 4 if i == 0 else 5)
            span(lambda p: sweep(i, 0, p, False), lo + 1, end - lo - 2, 3)
            near_wait(steps[i][0], near_send.at[i], near_recv.at[i])
            span(lambda p: cond(i, 0, p), end, NEAR, NEAR)
            span(lambda p: sweep(i, 0, p, False), end - 1, NEAR, NEAR)
            span(lambda p: cond(i, 1, p), lo + 1, end + 1 - lo, 3)
            span(lambda p: sweep(i, 1, p, False), lo + 2, end - 1 - lo, 4)
            span(lambda p: cond(i, 2, p), lo + 2, end - 1 - lo, 4)
            waits(i)
            span(lambda p: sweep(i, 2, p, False), lo + 3, end - 3 - lo, 5 if i == 0 else 2)

        early(0)

        def both():
            near_copy(U1, near_send.at[1], near_recv.at[1]).start()
            early(1)
        if second is True:
            both()
        else:
            pl.when(second)(both)
        hook()

        def wave(j, c):
            @pl.when(has_far)
            def _():
                copy = far_copy(U0, far_send, far_recv, j)
                copy.wait_send()
                copy.wait_recv()

            def part(i):
                p = first - 1 - 2 * j + SWEEPS * i
                for k in range(SWEEPS):
                    cond(i, k, p)
                    cond(i, k, p - 1)
                    p = p + 1
                    sweep(i, k, p, True)
                    sweep(i, k, p - 1, True)
            part(0)
            if second is True:
                part(1)
            else:
                pl.when(second)(lambda: part(1))
            return c
        lax.fori_loop(0, FAR // 2, wave, 0)

    def v_state(n):
        return V.at[n]

    def f_state(n):
        return F.at[n]

    def no_wait(i):
        pass

    def each(body):
        def one(z, c):
            body(z)
            return c
        lax.fori_loop(0, depth, one, 0)

    near_wait(KP.at[0], cf_s.at[0, FAR], cf_r.at[0, FAR])
    near_wait(HS.at[0], cf_s.at[1, FAR], cf_r.at[1, FAR])

    def coefficients():
        far_wait(KP.at[0], cf_s.at[0], cf_r.at[0], range(FAR // 2))
        far_wait(HS.at[0], cf_s.at[1], cf_r.at[1], range(FAR // 2))

        def scale(z, c):
            KP[1, z] = STEPS_DEV * KP[0, z]
            HS[1, z] = STEPS_DEV * HS[0, z]
            return c
        lax.fori_loop(0, top, scale, 0)

    def v_pair(n, coefs, terms, waits, hook):
        par = lax.rem(lax.div(n, 2), 2)
        pair(v_state, n, coefs, terms, waits, (vf_s.at[par], vf_r.at[par]), (vn_s, vn_r), hook, True)

    def v_send(n):
        par = lax.rem(lax.div(n, 2), 2)
        near_copy(V.at[n], vn_s.at[0], vn_r.at[0]).start()
        far_start(V.at[n], vf_s.at[par], vf_r.at[par])

    extra = 2 * STEPS_DEV + n_slab + 2

    def fine_pair(m, c):
        n = 2 * m + lax.div(m, STEPS_DEV) * (extra - 2 * STEPS_DEV)

        @pl.when(m > 0)
        def _():
            v_send(n)
        v_pair(n, (0, 0), (None, None), no_wait, lambda: pl.when(m == 0)(coefficients))

        @pl.when(m == STEPS_DEV // 2)
        def _():
            U = V.at[STEPS_DEV]
            span(lambda p: conduct(U, 1, 0, p), NEAR, top - NEAR, 4)
            span(lambda p: relax(U, U, 1, 0, p, T.at[0], None, True), NEAR + 1, top - NEAR - 2, 4)
            span(lambda p: conduct(T.at[0], 1, 1, p), NEAR + 1, top - NEAR - 2, 4)
            span(lambda p: relax(T.at[0], U, 1, 1, p, T.at[1], None, True), NEAR + 2, top - NEAR - 4, 4)
            span(lambda p: conduct(T.at[1], 1, 2, p), NEAR + 2, top - NEAR - 4, 4)
            span(lambda p: relax(T.at[1], U, 1, 2, p, T.at[2], None, False), first, depth, 4)

            def keep(z):
                CT[z] = T[2, own_lo + z]
            each(keep)
        return c
    lax.fori_loop(0, STEPS_DEV + lax.div(t, n_slab) * (1 - zh) * (STEPS_DEV // 2), fine_pair, 0)

    def rel_copy(n, tt, k):
        return remote(V.at[n, inner], REL, rel_s.at[k], rel_r, tt, s)

    def ct_copy(i, h):
        return remote(CT, CTB.at[i, pl.ds(own_lo - NEAR, depth)], ct_s.at[h], ct_r.at[i], n_slab + h, s)

    def halo_copy(i):
        par = lax.rem(i, 2)
        there = (1 - odd) * depth
        return remote(
            CTB.at[2 * i, pl.ds(lowest(FAR, NEAR) - NEAR, NEAR)], CTB.at[2 * i, pl.ds(there, NEAR)],
            th_s.at[par], th_r.at[par], t, far_s)

    def halo_start(i):
        ct_copy(2 * i, 0).wait_recv()

        @pl.when(has_far)
        def _():
            halo_copy(i).start()

    def bef_copy(n, i):
        return remote(V.at[n, inner], F.at[0, inner], bef_s.at[i, 0], bef_r, i, s)

    def own_copy(n, i):
        return remote(V.at[n, inner], OWN, bef_s.at[i, 1], own_r, i, s)

    begin = 2 * STEPS_DEV - 1

    def relay_in(n, i, k):
        return remote(V.at[n, inner], RB.at[k], bef_s.at[i, k], rb_r.at[k], i - lane_t, s)

    def relay_out(k):
        dst, recv = ((F.at[0, inner], bef_r), (OWN, own_r))[k]
        return remote(RB.at[k], dst, rl_s.at[k], recv, t + lane_t, s)

    def hand_out(d, n):
        d = jnp.asarray(d, jnp.int32)
        to_own = lax.rem(d + zh, 2) == 0
        for k, e, wanted in ((0, d + 1, jnp.logical_not(to_own)), (1, d, to_own)):
            wanted = wanted & (e < n_slab)
            by_relay = (e >= lane_t) & (e < 2 * lane_t)

            @pl.when(wanted & by_relay)
            def _():
                relay_in(n, e, k).start()

            @pl.when(wanted & jnp.logical_not(by_relay))
            def _():
                (bef_copy, own_copy)[k](n, e).start()

    def f_pair(n, par):
        near_copy(F.at[n], fn_s.at[0], fn_r.at[0]).start()
        far_start(F.at[n], ff_s.at[par], ff_r.at[par])
        pair(
            f_state, n, (0, 0), (None, None), no_wait, (ff_s.at[par], ff_r.at[par]), (fn_s, fn_r), lambda: None,
            par == 0)

    def f_both(c):
        def one(m, c):
            f_pair(2 * m, m)
            return c
        lax.fori_loop(0, 2, one, 0)

    def take(n):
        def one(z):
            F[0, own_lo + z] = V[n, own_lo + z]
        each(one)

    @pl.when(is_home)
    def _():
        hand_out(0, STEPS_DEV)

        @pl.when(zh == 0)
        def _():
            rel_copy(STEPS_DEV, 0, 0).start()
            rel_copy(extra + STEPS_DEV, t_next, 1).start()

    @pl.when(t == 0)
    def _():
        to_inside(u0[...], F.at[0], 1.0)

    @pl.when(is_home)
    def _():
        def advance(i, c):
            n = 2 * STEPS_DEV + 2 * i
            v_send(n)
            @pl.when(2 * i + 1 < n_slab - 1)
            def _():
                hand_out(2 * i + 1, n)

            @pl.when(i == 0)
            def _():
                halo_start(i)

            def release():
                for k in range(2):
                    @pl.when(2 * i + k + WINDOW < n_slab)
                    def _():
                        pl.semaphore_signal(
                            credit.at[zh], inc=1, device_id=(2 * i + k + WINDOW, s), device_id_type=MESH)

            def waits(k):
                if k == 0:
                    release()
                else:
                    ct_copy(2 * i + 1, 0).wait_recv()

            def hook():
                @pl.when(has_far)
                def _():
                    copy = halo_copy(i)
                    copy.wait_send()
                    copy.wait_recv()
            v_pair(n, (1, 1), (CTB.at[2 * i], CTB.at[2 * i + 1]), waits, hook)

            @pl.when(2 * i + 2 < n_slab)
            def _():
                halo_start(i + 1)
            hand_out(2 * i + 2, n + 1)
            return c
        lax.fori_loop(0, n_slab // 2, advance, 0)
        hand_out(n_slab - 1, begin + n_slab - 1)

        def last(z):
            OWN[z] = V[begin + n_slab + zh, own_lo + z]
        each(last)

    @pl.when(not_home)
    def _():
        def term(z):
            CT[z] = V[2 * STEPS_DEV, own_lo + z] - CT[z]
        each(term)
        for h in range(2):
            @pl.when(t >= WINDOW)
            def _():
                pl.semaphore_wait(credit.at[h], 1)
            ct_copy(t, h).start()

        @pl.when(t >= n_slab - STEPS_DEV)
        def _():
            rel_copy(STEPS_DEV, t_next, 0).start()

        @pl.when(t > 0)
        def _():
            bef_copy(0, t).wait_recv()

        @pl.when(t < n_slab - STEPS_DEV)
        def _():
            rel_copy(STEPS_DEV, t_next, 0).start()

    @pl.when(is_home)
    def _():
        take(begin + n_slab - 1 + zh)
    f_both(0)

    for i in range(STEPS_DEV - 1):
        to_outside(lambda z: F[i + 1, own_lo + z], fine.at[i])

    @pl.when(not_home)
    def _():
        own_copy(0, t).wait_recv()
    rel_copy(STEPS_DEV, t_next, 0).wait_recv()
    to_outside(lambda z: OWN[z], fine.at[STEPS_DEV - 1])
    to_outside(lambda z: OWN[z] - REL[z], pc.at[0])

    @pl.when(relays)
    def _():
        for k in range(2):
            relay_in(0, t + lane_t, k).wait_recv()
            relay_out(k).start()
        for k in range(2):
            relay_out(k).wait_send()

    @pl.when(not_home)
    def _():
        rel_copy(STEPS_DEV, t_next, 0).wait_send()
        for h in range(2):
            ct_copy(t, h).wait_send()

    @pl.when(t == n_slab)
    def _():
        for k in range(2):
            rel_copy(STEPS_DEV, 0, k).wait_send()

    @pl.when(is_home)
    def _():
        def one(i, c):
            @pl.when(lax.rem(i + zh, 2) == 0)
            def _():
                own_copy(0, i).wait_send()

                @pl.when(i > 0)
                def _():
                    bef_copy(0, i).wait_send()
            return c
        lax.fori_loop(0, n_slab, one, 0)


def solution(mesh):
    n_tm, n_sp = mesh.shape["tm"], mesh.shape["space"]

    def per_device(coarse_guess, initial, kappa, source):
        depth, nx, ny = initial.shape
        plane = (nx // 8, 8, ny)
        top = FAR + depth + NEAR
        n_terms = n_tm - 2
        dma = pltpu.SemaphoreType.DMA
        whole = pl.BlockSpec(memory_space=pltpu.VMEM)
        f32 = jnp.float32
        return pl.pallas_call(
            functools.partial(kernel, n_tm, n_sp),
            out_shape=(
                jax.ShapeDtypeStruct((STEPS_DEV, depth, nx, ny), f32),
                jax.ShapeDtypeStruct((1, depth, nx, ny), f32),
            ),
            in_specs=[whole] * 4,
            out_specs=(whole, whole),
            scratch_shapes=[
                pltpu.VMEM((3 * STEPS_DEV + 3 + n_terms, top) + plane, f32),
                pltpu.VMEM((STEPS_DEV + 1, top) + plane, f32),
                pltpu.VMEM((2, top) + plane, f32),
                pltpu.VMEM((2, top) + plane, f32),
                pltpu.VMEM((4, top) + plane, f32),
                pltpu.VMEM((2 * SWEEPS, top) + plane, f32),
                pltpu.VMEM((2 * SWEEPS, top) + plane, f32),
                pltpu.VMEM((2, depth, nx, ny // 2), f32),
                pltpu.VMEM((depth,) + plane, f32),
                pltpu.VMEM((n_terms, depth + NEAR) + plane, f32),
                pltpu.VMEM((depth,) + plane, f32),
                pltpu.VMEM((depth,) + plane, f32),
                pltpu.VMEM((2, depth) + plane, f32),
                dma((2, FAR + 1)), dma((2, FAR + 1)),
                dma((2, FAR)), dma((2, FAR)), dma((2,)), dma((2,)),
                dma((2, FAR)), dma((2, FAR)), dma((2,)), dma((2,)),
                dma((2,)), dma, dma((n_tm, 2)), dma, dma, dma((2,)), dma((n_tm,)), dma((2,)), dma((2,)), dma((2,)), dma((2,)),
                pltpu.SemaphoreType.REGULAR((2,)),
            ],
            compiler_params=pltpu.CompilerParams(
                collective_id=0, has_side_effects=True, vmem_limit_bytes=56 * 1024 * 1024
            ),
        )(coarse_guess, initial, kappa, source)

    return jax.shard_map(
        per_device,
        mesh=mesh,
        in_specs=(
            P("tm", "space", None, None),
            P("space", None, None),
            P("space", None, None),
            P("space", None, None),
        ),
        out_specs=(P("tm", "space", None, None), P("tm", "space", None, None)),
        check_vma=False,
    )
```
